256 devices in a mesh: sector: 16 (over y, x_hi, core), dof: 16 (over z, x_lo).
Axes of the slice: x: 4 (x_hi: 2, x_lo: 2; x = x_hi * 2 + x_lo), y: 4, z: 8, core: 2. Of those that a mesh axis runs over, the one named last changes fastest.
Arguments:
- adjoint_start: float32 [2, 32, 49152], P(None, 'sector', 'dof'), may hold values from -4 to 4
- right_side: float32 [2, 32, 49152], P(None, 'sector', 'dof'), may hold values from -6 to 6
- response: float32 [2, 32, 49152], P(None, 'sector', 'dof'), may hold values from -1 to 1
- stiffness: float32 [768, 3, 64, 64], P('dof'), may hold values from -0.4375 to 0.4375
- block_cols: int32 [768, 3], P('dof'), may hold values from 0 to 767, as said below
- coupling: float32 [768, 64, 64], P('dof'), may hold values from -0.75 to 0.75
- tile_table: float32 [32, 64, 64], replicated, may hold values from -0.75 to 0.75
- tile_ids: int32 [32, 768], P('sector', 'dof'), may hold values from 0 to 31
- mistune: float32 [32, 768], P('sector', 'dof'), may hold values from 0.25 to 2
- inverses: float32 [32, 768, 64, 64], P('sector', 'dof'), may hold values from -0.75 to 0.75
Outputs:
- adjoint: float32 [2, 32, 49152], P(None, 'sector', 'dof')
- residual: float32 [2, 32, 49152], P(None, 'sector', 'dof')
- sensitivity: float32 [32, 768], P('sector', 'dof')
The draws below stay inside these ranges and needn't reach their ends.
Inputs may be any that keep to these rules, and one draw needn't show every extreme that they name: block_cols[b, 0] is b; every other slot differs from b by 1 to 3 blocks, and the distance 3 occurs.
All inputs are finite; a program needn't handle non-finite values.
Results may differ from the reference program's by a relative error of at most 0.00011.
Values sent between devices are 32-bit elements; how exact they have to be, the bound alone decides.
A program may use at most 128 MiB of HBM per device.

```python
import math
import jax
import jax.numpy as jnp
from jax import lax

SECTORS = 32
BLK = 64
LOADS = 2
SLOTS = 3
REACH = 3
NTILE = 32
ITERS = 2
NBLOCKS = 768
NDOF = 49152


def draw_block_cols(key, part):
    key_reach, key_sign = jax.random.split(jax.random.fold_in(key, 11))
    row_index = jnp.arange(NBLOCKS, dtype=jnp.int32)[:, None]
    reach_draw = jax.random.randint(key_reach, (NBLOCKS, SLOTS - 1), 1, REACH + 1)
    slot_index = jnp.arange(SLOTS - 1, dtype=jnp.int32)[None, :]
    forced = jnp.where((row_index % 5 == 0) & (slot_index == 0), REACH, reach_draw)
    sign_draw = jax.random.randint(key_sign, (NBLOCKS, SLOTS - 1), 0, 2) * 2 - 1
    offsets = forced * sign_draw
    target = row_index + offsets
    target = jnp.where((target < 0) | (target >= NBLOCKS), row_index - offsets, target)
    return jnp.concatenate([row_index, target], axis=1).astype(jnp.int32)


def touch_ends(result, own_key, smallest, largest):
    longest = result.shape.index(max(result.shape))
    spots = []
    for shift in (0, 1):
        where = [jax.random.randint(jax.random.fold_in(own_key, axis), (), 0, length) for axis, length in enumerate(result.shape)]
        where[longest] = (where[longest] + shift) % result.shape[longest]
        spots.append(tuple(where))
    return result.at[spots[0]].set(smallest).at[spots[1]].set(largest)


def steps_of(stream_key, dims, pieces, smallest, high):
    loudness = 1.0
    for position, parts in pieces:
        draws = jax.random.uniform(jax.random.fold_in(jax.random.fold_in(stream_key, 6), position), (parts,), jnp.float32, smallest / len(pieces), high / len(pieces))
        loudness = loudness * jnp.repeat(jnp.exp(draws), dims[position] // parts).reshape((-1,) + (1,) * (len(dims) - 1 - position))
    return loudness


def gaussian(rng, dims, spread, most, pieces=(), kind=jnp.bfloat16):
    level = steps_of(rng, dims, pieces, -0.22, 0.18) if pieces else 1.0
    array = jax.random.normal(rng, dims, jnp.float32) * spread * level
    return jnp.minimum(jnp.maximum(array, -most), most).astype(kind)


def setup_inputs(seed: int = 0) -> dict:
    arg_keys = jax.random.split(jax.random.key(seed), 11)
    return {
        "adjoint_start": gaussian(arg_keys[0], (LOADS, SECTORS, NDOF), 0.5, 4.0, ((1, 16), (2, 16)), jnp.float32),
        "right_side": gaussian(arg_keys[1], (LOADS, SECTORS, NDOF), 1.0, 6.0, ((1, 16), (2, 16)), jnp.float32),
        "response": gaussian(arg_keys[2], (LOADS, SECTORS, NDOF), 0.125, 1.0, ((1, 16), (2, 16)), jnp.float32),
        "stiffness": gaussian(arg_keys[3], (NBLOCKS, SLOTS, BLK, BLK), (SLOTS * BLK) ** -0.5, 0.4375, ((0, 16),), jnp.float32),
        "block_cols": draw_block_cols(jax.random.fold_in(arg_keys[10], 71), 0),
        "coupling": gaussian(arg_keys[5], (NBLOCKS, BLK, BLK), BLK ** -0.5, 0.75, ((0, 16),), jnp.float32),
        "tile_table": gaussian(arg_keys[6], (NTILE, BLK, BLK), BLK ** -0.5, 0.75, (), jnp.float32),
        "tile_ids": touch_ends(jax.random.randint(arg_keys[7], (SECTORS, NBLOCKS), 0, NTILE), jax.random.fold_in(arg_keys[7], 1), 0, NTILE - 1).astype(jnp.int32),
        "mistune": jnp.clip(jnp.exp(math.log(2.0) - 2.0794415 * jax.random.uniform(arg_keys[8], (SECTORS, NBLOCKS), jnp.float32) ** steps_of(arg_keys[8], (SECTORS, NBLOCKS), ((0, 16), (1, 16)), -0.2, 0.2)), 0.25, 2.0),
        "inverses": gaussian(arg_keys[9], (SECTORS, NBLOCKS, BLK, BLK), BLK ** -0.5, 0.75, ((0, 16), (1, 16)), jnp.float32),
    }


highest = lax.Precision.HIGHEST

def hartley(row_index, col_index, period):
    product = row_index[:, None] * col_index[None, :] % period
    phase_angle = product.astype(jnp.float32) * (2.0 * math.pi / period)
    return (jnp.cos(phase_angle) + jnp.sin(phase_angle)) / math.sqrt(period)

def operate(vector, stiffness, block_cols, coupling, tile_table, tile_ids, mistune):
    load_count, sector_count, dof_count = vector.shape
    blocks = vector.reshape(load_count, sector_count, NBLOCKS, BLK)
    picked = blocks[:, :, block_cols, :]
    banded = jnp.einsum('bpij,lsbpj->lsbi', stiffness, picked, precision=highest)
    nearby = jnp.roll(blocks, 1, axis=1) + jnp.roll(blocks, -1, axis=1)
    coupled = jnp.einsum('bij,lsbj->lsbi', coupling, nearby, precision=highest)

    def one_sector(packed):
        ids_row, scale_row, sector_blocks = packed
        sector_tiles = tile_table[ids_row] * scale_row[:, None, None]
        return jnp.einsum('bij,lbj->lbi', sector_tiles, sector_blocks, precision=highest)
    perturbed = lax.map(one_sector, (tile_ids, mistune, jnp.moveaxis(blocks, 1, 0)))
    combined = banded + coupled + jnp.moveaxis(perturbed, 0, 1)
    return combined.reshape(load_count, sector_count, dof_count)

def precondition(residual, inverses):
    load_count = residual.shape[0]
    index = jnp.arange(SECTORS, dtype=jnp.int32)
    transform = hartley(index, index, SECTORS)
    spectrum = jnp.einsum('hs,lsn->lhn', transform, residual, precision=highest)
    spectrum = spectrum.reshape(load_count, SECTORS, NBLOCKS, BLK)
    solved = jnp.einsum('hbij,lhbj->lhbi', inverses, spectrum, precision=highest)
    solved = solved.reshape(load_count, SECTORS, NDOF)
    return jnp.einsum('hs,lhn->lsn', transform, solved, precision=highest)

def reference(adjoint_start, right_side, response, stiffness, block_cols, coupling, tile_table, tile_ids, mistune, inverses):
    adjoint = adjoint_start
    residual = right_side
    for iteration in range(ITERS):
        residual = right_side - operate(adjoint, stiffness, block_cols, coupling, tile_table, tile_ids, mistune)
        adjoint = adjoint + precondition(residual, inverses)
    load_count = adjoint.shape[0]
    adjoint_blocks = jnp.moveaxis(adjoint.reshape(load_count, SECTORS, NBLOCKS, BLK), 1, 0)
    response_blocks = jnp.moveaxis(response.reshape(load_count, SECTORS, NBLOCKS, BLK), 1, 0)

    def one_sector(packed):
        ids_row, scale_row, adjoint_part, response_part = packed
        sector_tiles = tile_table[ids_row] * scale_row[:, None, None]
        forced = jnp.einsum('bij,lbj->lbi', sector_tiles, response_part, precision=highest)
        return -lax.optimization_barrier(jnp.sum(adjoint_part * forced, axis=(0, 2)))
    sensitivity = lax.map(one_sector, (tile_ids, mistune, adjoint_blocks, response_blocks))
    return (adjoint, residual, sensitivity)
```

```python
import functools
import math

import jax
import jax.numpy as jnp
from jax import lax
from jax.experimental import pallas as pl
from jax.experimental.pallas import tpu as pltpu
from jax.sharding import PartitionSpec as P

ITERS = 2
NS = 16
PAIRS = 24
GROUPS = 8
EXT = 2
F32 = jnp.float32
BF16 = jnp.bfloat16


def row_iota():
    return lax.broadcasted_iota(jnp.int32, (8, 128), 0)


def lane_iota():
    return lax.broadcasted_iota(jnp.int32, (8, 128), 1)


def rolled(x, shift):
    shift = shift % 8
    return pltpu.roll(x, shift, axis=0) if shift else x


def half_rolled(x):
    return pltpu.roll(x, 64, axis=1)


def hartley16(values):
    count = len(values)
    if count == 1:
        return values
    even, odd = hartley16(values[0::2]), hartley16(values[1::2])
    half = count // 2
    low, high = [], []
    for k in range(half):
        angle = 2.0 * math.pi * k / count
        if k == 0:
            twist = odd[0]
        elif 4 * k == count:
            twist = odd[(half - k) % half]
        else:
            twist = math.cos(angle) * odd[k] + math.sin(angle) * odd[half - k]
        low.append(even[k] + twist)
        high.append(even[k] - twist)
    return low + high


def hartley32(values):
    is_even = row_iota() % 2 == 0
    y = hartley16(values)
    twisted = []
    for k in range(16):
        angle = 2.0 * math.pi * k / 32
        if k == 0:
            twisted.append(y[0])
        else:
            twisted.append(math.cos(angle) * y[k] + math.sin(angle) * y[16 - k])
    low, high = [], []
    for j in range(8):
        a = jnp.where(is_even, y[2 * j], rolled(y[2 * j + 1], 1))
        b = jnp.where(is_even, rolled(twisted[2 * j], 7), twisted[2 * j + 1])
        low.append(a + b)
        high.append(a - b)
    return low + high


def unpacked(c0, c1, r):
    row = row_iota()
    part = jnp.where(row < 2, rolled(c0, -2 * r), rolled(c1, 2 - 2 * r))
    part = jnp.where(row < 4, part, 0.0)
    return part + rolled(part, 4)


def packed(p0, p1, p2):
    g = row_iota() // 2
    zero = jnp.zeros((8, 128), F32)
    c0 = jnp.where(g == 0, p0, jnp.where(g == 1, rolled(p1, 2), jnp.where(g == 2, p2, zero)))
    c1 = jnp.where(g == 0, rolled(p0, 6), jnp.where(g == 1, p1, jnp.where(g == 2, rolled(p2, 6), zero)))
    return c0, c1


def halves(x):
    high = x.astype(BF16).astype(F32)
    return high, x - high


def matmul_t(a, b):
    return lax.dot_general(a, b, (((1,), (1,)), ((), ())), preferred_element_type=F32)


def own_block_product(pair, weights):
    row, lane = row_iota(), lane_iota()
    own = (row < 4) == (lane < 64)
    high, low = halves(pair)
    chunks = []
    for s in range(2):
        mask = jnp.where(own, (row % 2 == s).astype(F32), 0.0)
        chunks.append(jnp.concatenate([high * mask, low * mask], axis=0).astype(BF16))
    out = matmul_t(jnp.concatenate(chunks, axis=1), weights)
    total = out[:8] + out[8:]
    total = total + half_rolled(total)
    return jnp.where(own, total, rolled(total, 4))


def kernel(
    dof_count,
    v0_hbm, rs_hbm, resp_hbm, cols_hbm, ids_hbm, mist_hbm, stiff_ref, coup_ref, tile_ref, inv_ref,
    adj_ref, res_ref, sens_ref,
    v0_ref, rs_ref, resp_ref, cols_ref, ids_ref, mist_ref,
    stiff, coup, tiles, inv, w_main, w_tile, w_inv,
    adj, right, forced, near, vdup, vpair, tile_part,
    halo_s, halo_d, buf, buf_near, snd, snd_near,
    local_sem, hs_send, hs_recv, hd_send, hd_recv, a_send, a_recv,
):
    me = lax.axis_index("sector")
    dof = lax.axis_index("dof")
    nxt, prv = lax.rem(me + 1, NS), lax.rem(me + NS - 1, NS)
    dup, ddn = lax.rem(dof + 1, dof_count), lax.rem(dof + dof_count - 1, dof_count)
    row, lane = row_iota(), lane_iota()
    is_even = row % 2 == 0
    left_half = lane < 64

    loads = [
        pltpu.make_async_copy(tile_ref, tiles, local_sem.at[0]),
        pltpu.make_async_copy(stiff_ref, stiff, local_sem.at[1]),
        pltpu.make_async_copy(coup_ref, coup, local_sem.at[2]),
        pltpu.make_async_copy(inv_ref, inv, local_sem.at[3]),
        pltpu.make_async_copy(v0_hbm, v0_ref, local_sem.at[4]),
        pltpu.make_async_copy(rs_hbm, rs_ref, local_sem.at[5]),
        pltpu.make_async_copy(resp_hbm, resp_ref, local_sem.at[6]),
        pltpu.make_async_copy(cols_hbm, cols_ref, local_sem.at[7]),
        pltpu.make_async_copy(ids_hbm, ids_ref, local_sem.at[8]),
        pltpu.make_async_copy(mist_hbm, mist_ref, local_sem.at[9]),
    ]
    for i in (4, 5, 6, 8, 9, 0, 1, 2, 7, 3):
        loads[i].start()

    barrier = pltpu.get_barrier_semaphore()

    def greet(step, carry):
        pl.semaphore_signal(barrier, inc=1, device_id={"sector": lax.rem(me + step, NS)})
        return carry

    lax.fori_loop(1, NS, greet, 0)
    pl.semaphore_signal(barrier, inc=1, device_id={"dof": dup})
    pl.semaphore_signal(barrier, inc=1, device_id={"dof": ddn})

    zero2 = jnp.zeros((2, 128), F32)
    for i, source, target in ((4, v0_ref, adj), (5, rs_ref, right), (6, resp_ref, forced)):
        loads[i].wait()
        for q in range(GROUPS):
            for l in range(2):
                for c in range(3):
                    target[2 * q + l, 2 * c : 2 * c + 2, :] = source[l, :, 128 * (3 * q + c) : 128 * (3 * q + c + 1)]
                target[2 * q + l, 6:8, :] = zero2

    pl.semaphore_wait(barrier, NS + 1)

    def sector_halo():
        return [
            pltpu.make_async_remote_copy(adj, halo_s.at[1], hs_send.at[0], hs_recv.at[1], device_id={"sector": prv}),
            pltpu.make_async_remote_copy(adj, halo_s.at[0], hs_send.at[1], hs_recv.at[0], device_id={"sector": nxt}),
        ]

    def dof_halo(it):
        return [
            pltpu.make_async_remote_copy(
                adj.at[14:16], halo_d.at[it, 0], hd_send.at[it, 0], hd_recv.at[it, 0], device_id={"dof": dup}
            ),
            pltpu.make_async_remote_copy(
                adj.at[0:2], halo_d.at[it, 1], hd_send.at[it, 1], hd_recv.at[it, 1], device_id={"dof": ddn}
            ),
        ]

    halos = sector_halo()
    for copy in halos:
        copy.start()

    def start_all_to_all(source, target, phase):
        def send(step, carry):
            k = lax.rem(me + step, NS)
            pltpu.make_async_remote_copy(
                source.at[k], target.at[me], a_send.at[phase], a_recv.at[phase], device_id={"sector": k}
            ).start()
            return carry

        lax.fori_loop(1, NS, send, 0)
        target[me] = source[me]

    def finish_all_to_all(source, target, phase):
        pltpu.make_async_copy(target.at[0 : NS - 1], target.at[0 : NS - 1], a_recv.at[phase]).wait()

    def split_store(target, c, base, lanes, value):
        high = value.astype(BF16)
        target[c, base : base + 64, lanes] = high
        target[c, base + 64 : base + 128, lanes] = (value - high.astype(F32)).astype(BF16)

    def prepare_tiles(c, carry):
        for s in range(2):
            parts = [tiles[ids_ref[s, 2 * c + b]] * mist_ref[s, 2 * c + b] for b in range(2)]
            split_store(w_tile, c, 0, slice(128 * s, 128 * s + 128), jnp.concatenate(parts, axis=1))
        return carry

    def prepare_inverses(c, carry):
        for s in range(2):
            parts = [inv[s, 2 * c + b] for b in range(2)]
            split_store(w_inv, c, 0, slice(128 * s, 128 * s + 128), jnp.concatenate(parts, axis=1))
        return carry

    def prepare_main(c, carry):
        for b in range(2):
            mats = [[stiff[2 * c + b, 0], stiff[2 * c + b, 1]], [coup[2 * c + b], stiff[2 * c + b, 2]]]
            for chunk in range(2):
                pair = mats[chunk] if b == 0 else mats[chunk][::-1]
                split_store(
                    w_main, c, 128 * b, slice(128 * chunk, 128 * chunk + 128), jnp.concatenate(pair, axis=1)
                )
        return carry

    def spread(pair, position):
        high, low = halves(pair)
        value = jnp.where(row < 4, high, low)
        turned = half_rolled(value)
        vdup[2 * position] = jnp.where(left_half, value, turned)
        vdup[2 * position + 1] = jnp.where(left_half, turned, value)
        return value

    def own_part(q, carry):
        c0, c1 = adj[2 * q], adj[2 * q + 1]
        for r in range(3):
            c = 3 * q + r
            pair = unpacked(c0, c1, r)
            vpair[c] = spread(pair, c + EXT)
            tile_part[c] = own_block_product(pair, w_tile[c])
        return carry

    def halo_part(it):
        for r in range(1, 3):
            spread(unpacked(halo_d[it, 0, 0], halo_d[it, 0, 1], r), r - 1)
        for r in range(2):
            spread(unpacked(halo_d[it, 1, 0], halo_d[it, 1, 1], r), PAIRS + EXT + r)

    first_block = dof * (2 * PAIRS) - 2 * EXT

    def neighbour_part(it, q, carry):
        n0, n1 = near[2 * q], near[2 * q + 1]
        pairs = []
        for r in range(3):
            c = 3 * q + r
            high, low = halves(unpacked(n0, n1, r))
            nearby = jnp.where(row < 4, high, low)
            own = vpair[c]
            chunk_a, chunk_b = [], []
            for b in range(2):
                x1 = vdup[jnp.maximum(cols_ref[1, 2 * c + b] - first_block, 0)]
                x2 = vdup[jnp.maximum(cols_ref[2, 2 * c + b] - first_block, 0)]
                here = left_half if b == 0 else jnp.logical_not(left_half)
                chunk_a.append(jnp.where(here, own, x1))
                chunk_b.append(jnp.where(here, nearby, x2))
            lhs = jnp.concatenate([jnp.concatenate(chunk_a, axis=0), jnp.concatenate(chunk_b, axis=0)], axis=1)
            out = matmul_t(lhs.astype(BF16), w_main[c])
            o0, o1 = out[:8, :128], out[8:, 128:]
            total = jnp.where(left_half, o0, o1) + half_rolled(jnp.where(left_half, o1, o0))
            pairs.append(total + rolled(total, 4) + tile_part[c])
        c0, c1 = packed(*pairs)
        snd[3 * it, 2 * q] = right[2 * q] - c0
        snd[3 * it, 2 * q + 1] = right[2 * q + 1] - c1
        return carry

    def forced_part(q, carry):
        c0, c1 = forced[2 * q], forced[2 * q + 1]
        c0, c1 = packed(*[own_block_product(unpacked(c0, c1, r), w_tile[3 * q + r]) for r in range(3)])
        forced[2 * q], forced[2 * q + 1] = c0, c1
        return carry

    def solve_part(it, q, carry):
        c0, c1 = buf[3 * it + 1, 2 * q], buf[3 * it + 1, 2 * q + 1]
        c0, c1 = packed(*[own_block_product(unpacked(c0, c1, r), w_inv[3 * q + r]) for r in range(3)])
        snd[3 * it + 2, 2 * q], snd[3 * it + 2, 2 * q + 1] = c0, c1
        return carry

    loads[8].wait()
    loads[9].wait()
    loads[0].wait()
    for it in range(ITERS):
        dofs = dof_halo(it)
        for copy in dofs:
            copy.start()
        if it == 0:
            lax.fori_loop(0, PAIRS, prepare_tiles, 0)
        lax.fori_loop(0, GROUPS, own_part, 0)
        if it == 0:
            loads[1].wait()
            loads[2].wait()
            loads[7].wait()
            lax.fori_loop(0, PAIRS, prepare_main, 0)
            for copy in halos:
                copy.wait_recv()
            for k in range(NS):
                below, above = halo_s[0, k] + adj[k], adj[k] + halo_s[1, k]
                near[k] = jnp.where(is_even, rolled(below, 7), rolled(above, 1))
        for copy in dofs:
            copy.wait_recv()
        halo_part(it)
        lax.fori_loop(0, GROUPS, functools.partial(neighbour_part, it), 0)

        start_all_to_all(snd.at[3 * it], buf.at[3 * it], 4 * it)
        if it == 0:
            loads[3].wait()
            lax.fori_loop(0, PAIRS, prepare_inverses, 0)
        else:
            for q in range(GROUPS):
                for l in range(2):
                    for c in range(3):
                        res_ref[l, :, 128 * (3 * q + c) : 128 * (3 * q + c + 1)] = snd[
                            3 * it, 2 * q + l, 2 * c : 2 * c + 2, :
                        ]
        finish_all_to_all(snd.at[3 * it], buf.at[3 * it], 4 * it)
        spectrum = hartley32([buf[3 * it, j] for j in range(NS)])
        for j in range(NS):
            snd[3 * it + 1, j] = spectrum[j]

        start_all_to_all(snd.at[3 * it + 1], buf.at[3 * it + 1], 4 * it + 1)
        if it == 0:
            lax.fori_loop(0, GROUPS, forced_part, 0)
        finish_all_to_all(snd.at[3 * it + 1], buf.at[3 * it + 1], 4 * it + 1)
        lax.fori_loop(0, GROUPS, functools.partial(solve_part, it), 0)

        start_all_to_all(snd.at[3 * it + 2], buf.at[3 * it + 2], 4 * it + 2)
        finish_all_to_all(snd.at[3 * it + 2], buf.at[3 * it + 2], 4 * it + 2)
        update = hartley32([buf[3 * it + 2, j] * (1.0 / 32.0) for j in range(NS)])
        if it == 0:
            sums = [update[j] + update[(j + 1) % NS] for j in range(NS)]
            for j in range(NS):
                snd_near[j, 0] = update[j]
                snd_near[j, 1] = jnp.where(is_even, rolled(sums[j - 1], 7), rolled(sums[j], 1))
            start_all_to_all(snd_near, buf_near, 4 * it + 3)
            for copy in halos + dofs:
                copy.wait_send()
            finish_all_to_all(snd_near, buf_near, 4 * it + 3)
            for k in range(NS):
                adj[k] += buf_near[k, 0]
                near[k] += buf_near[k, 1]
        else:
            for j in range(NS):
                snd[6, j] = update[j]
            start_all_to_all(snd.at[6], buf.at[6], 4 * it + 3)
            for copy in dofs:
                copy.wait_send()
            finish_all_to_all(snd.at[6], buf.at[6], 4 * it + 3)
            for k in range(NS):
                adj[k] += buf[6, k]

    for q in range(GROUPS):
        c0, c1 = adj[2 * q], adj[2 * q + 1]
        for l, chunk in ((0, c0), (1, c1)):
            for c in range(3):
                adj_ref[l, :, 128 * (3 * q + c) : 128 * (3 * q + c + 1)] = chunk[2 * c : 2 * c + 2, :]
        product = c0 * forced[2 * q] + c1 * forced[2 * q + 1]
        first = jnp.sum(jnp.where(left_half, product, 0.0), axis=1, keepdims=True)
        second = jnp.sum(jnp.where(left_half, 0.0, product), axis=1, keepdims=True)
        sens_ref[q] = -jnp.where(lane == 0, first, second)

    for phase in range(4 * ITERS):
        part = snd_near.at[0 : NS - 1] if phase == 3 else snd.at[0, 0 : NS - 1]
        pltpu.make_async_copy(part, part, a_send.at[phase]).wait()


def body(dof_count, adjoint_start, right_side, response, stiffness, block_cols, coupling, tile_table, tile_ids, mistune, inverses):
    vmem = pl.BlockSpec(memory_space=pltpu.VMEM)
    hbm = pl.BlockSpec(memory_space=pltpu.HBM)
    chunks = (NS, 8, 128)
    adjoint, residual, sens = pl.pallas_call(
        functools.partial(kernel, dof_count),
        out_shape=(
            jax.ShapeDtypeStruct(adjoint_start.shape, F32),
            jax.ShapeDtypeStruct(adjoint_start.shape, F32),
            jax.ShapeDtypeStruct((GROUPS, 8, 128), F32),
        ),
        in_specs=[hbm] * 10,
        out_specs=(vmem, vmem, vmem),
        scratch_shapes=[
            pltpu.VMEM(adjoint_start.shape, F32),
            pltpu.VMEM(adjoint_start.shape, F32),
            pltpu.VMEM(adjoint_start.shape, F32),
            pltpu.SMEM(block_cols.shape[::-1], jnp.int32),
            pltpu.SMEM(tile_ids.shape, jnp.int32),
            pltpu.SMEM(mistune.shape, F32),
            pltpu.VMEM(stiffness.shape, F32),
            pltpu.VMEM(coupling.shape, F32),
            pltpu.VMEM(tile_table.shape, F32),
            pltpu.VMEM(inverses.shape, F32),
            pltpu.VMEM((PAIRS, 256, 256), BF16),
            pltpu.VMEM((PAIRS, 128, 256), BF16),
            pltpu.VMEM((PAIRS, 128, 256), BF16),
            pltpu.VMEM(chunks, F32),
            pltpu.VMEM(chunks, F32),
            pltpu.VMEM(chunks, F32),
            pltpu.VMEM(chunks, F32),
            pltpu.VMEM((2 * (PAIRS + 2 * EXT), 8, 128), F32),
            pltpu.VMEM((PAIRS, 8, 128), F32),
            pltpu.VMEM((PAIRS, 8, 128), F32),
            pltpu.VMEM((2,) + chunks, F32),
            pltpu.VMEM((ITERS, 2, 2, 8, 128), F32),
            pltpu.VMEM((7,) + chunks, F32),
            pltpu.VMEM((NS, 2, 8, 128), F32),
            pltpu.VMEM((7,) + chunks, F32),
            pltpu.VMEM((NS, 2, 8, 128), F32),
            pltpu.SemaphoreType.DMA((10,)),
            pltpu.SemaphoreType.DMA((2,)),
            pltpu.SemaphoreType.DMA((2,)),
            pltpu.SemaphoreType.DMA((ITERS, 2)),
            pltpu.SemaphoreType.DMA((ITERS, 2)),
            pltpu.SemaphoreType.DMA((4 * ITERS,)),
            pltpu.SemaphoreType.DMA((4 * ITERS,)),
        ],
        compiler_params=pltpu.CompilerParams(collective_id=0, has_side_effects=True, vmem_limit_bytes=60 * 1024 * 1024),
    )(
        adjoint_start, right_side, response, block_cols.T, tile_ids, mistune, stiffness, coupling, tile_table, inverses
    )
    sens = sens[:, :6, :2].reshape(GROUPS, 3, 2, 2).transpose(2, 0, 1, 3).reshape(2, 2 * PAIRS)
    return adjoint, residual, sens


def solution(mesh):
    in_specs = (
        P(None, "sector", "dof"),
        P(None, "sector", "dof"),
        P(None, "sector", "dof"),
        P("dof", None, None, None),
        P("dof", None),
        P("dof", None, None),
        P(),
        P("sector", "dof"),
        P("sector", "dof"),
        P("sector", "dof", None, None),
    )
    out_specs = (P(None, "sector", "dof"), P(None, "sector", "dof"), P("sector", "dof"))
    run = functools.partial(body, mesh.shape["dof"])
    return jax.shard_map(run, mesh=mesh, in_specs=in_specs, out_specs=out_specs, check_vma=False)
```

```python
import functools
import math

import jax
import jax.numpy as jnp
from jax import lax
from jax.experimental import pallas as pl
from jax.experimental.pallas import tpu as pltpu
from jax.sharding import PartitionSpec as P

ITERS = 2
NS = 16
OWN = 3
PAIRS = 24
MSG = 32
F32 = jnp.float32
BF16 = jnp.bfloat16


def iota(rows, axis):
    return lax.broadcasted_iota(jnp.int32, (rows, 128), axis)


def rolled(x, shift):
    return pltpu.roll(x, shift, axis=0)


def turned(x):
    return pltpu.roll(x, 64, axis=1)


def hartley16(values):
    count = len(values)
    if count == 1:
        return values
    even, odd = hartley16(values[0::2]), hartley16(values[1::2])
    half = count // 2
    low, high = [], []
    for k in range(half):
        angle = 2.0 * math.pi * k / count
        if k == 0:
            twist = odd[0]
        elif 4 * k == count:
            twist = odd[half - k]
        else:
            twist = math.cos(angle) * odd[k] + math.sin(angle) * odd[half - k]
        low.append(even[k] + twist)
        high.append(even[k] - twist)
    return low + high


def hartley32(values):
    is_even = iota(8, 0) % 2 == 0
    y = hartley16(values)
    twisted = [y[0]]
    for k in range(1, 16):
        angle = 2.0 * math.pi * k / 32
        twisted.append(math.cos(angle) * y[k] + math.sin(angle) * y[16 - k])
    low, high = [], []
    for j in range(8):
        a = jnp.where(is_even, y[2 * j], rolled(y[2 * j + 1], 1))
        b = jnp.where(is_even, rolled(twisted[2 * j], 7), twisted[2 * j + 1])
        low.append(a + b)
        high.append(a - b)
    return low + high


def halves(x):
    high = x.astype(BF16).astype(F32)
    return high, x - high


def matmul_t(a, b):
    return lax.dot_general(a, b, (((1,), (1,)), ((), ())), preferred_element_type=F32)


def own_product(x, weights):
    own = (iota(8, 1) // 64) == (iota(8, 0) % 2)
    high0, low0 = halves(jnp.where(own, x, 0.0))
    high1, low1 = halves(jnp.where(own, turned(x), 0.0))
    rows = jnp.concatenate([high0, high1, low0, low1], axis=0)
    block = (iota(32, 0) % 8) // 2
    lhs = [jnp.where(block == c, rows, 0.0).astype(BF16) for c in range(OWN)]
    out = matmul_t(jnp.concatenate(lhs, axis=1), weights)
    first, second = out[0:8] + out[16:24], out[8:16] + out[24:32]
    return jnp.where(own, first + turned(first), second + turned(second))


def kernel(
    dof_count,
    v0_hbm, rs_hbm, resp_hbm, cols_hbm, ids_hbm, mist_hbm, stiff_hbm, coup_hbm, tile_hbm, inv_hbm,
    fin_ref, res_ref,
    v0, rs, resp, cols, tiles, stiff, coup, inv,
    ids_all, mist_all, ids, mist,
    msg_out, msg, edge, packed, bulk,
    w_table, w_tile, w_inv, w_main,
    adj, right, forced, scale, work, acc, wide, near,
    halo_out, halo_low, halo_high, res_out, fin_out,
    local_sem, ids_sem, mist_sem, msg_sem, edge_send, edge_recv, bulk_send, bulk_recv,
    halo_send, halo_recv, res_sem, fin_sem,
):
    me = lax.axis_index("sector")
    dof = lax.axis_index("dof")
    dof_up, dof_down = lax.rem(dof + 1, dof_count), lax.rem(dof + dof_count - 1, dof_count)
    up = {"sector": lax.rem(me + 1, NS), "dof": lax.rem(dof + (me + 1) // NS, dof_count)}
    down = {
        "sector": lax.rem(me + NS - 1, NS),
        "dof": lax.rem(dof + dof_count - 1 + (me + NS - 1) // NS, dof_count),
    }

    mine = pl.ds(OWN * me, OWN)
    loads = [
        pltpu.make_async_copy(source, target, local_sem.at[i])
        for i, (source, target) in enumerate(
            (
                (v0_hbm, v0),
                (rs_hbm, rs),
                (resp_hbm, resp),
                (inv_hbm, inv),
                (tile_hbm, tiles),
                (stiff_hbm.at[mine], stiff),
                (coup_hbm.at[mine], coup),
                (cols_hbm, cols),
                (ids_hbm, ids_all.at[me]),
                (mist_hbm, mist_all.at[me]),
            )
        )
    ]
    for load in loads:
        load.start()

    barrier = pltpu.get_barrier_semaphore()

    def greet(step, carry):
        pl.semaphore_signal(barrier, inc=1, device_id={"sector": lax.rem(me + step, NS)})
        return carry

    lax.fori_loop(1, NS, greet, 0)

    def greet_row(row):
        def one(step, carry):
            pl.semaphore_signal(barrier, inc=1, device_id={"sector": step, "dof": row})
            return carry

        lax.fori_loop(0, NS, one, 0)

    @pl.when(me == 0)
    def _():
        greet_row(dof_down)

    @pl.when(me == NS - 1)
    def _():
        greet_row(dof_up)

    left2 = iota(2, 1) < 64
    for base, field, i in ((0, v0, 0), (6, rs, 1), (12, resp, 2)):
        loads[i].wait()
        for p in range(PAIRS):
            lanes = slice(128 * p, 128 * p + 128)
            a, b = field[0, :, lanes], field[1, :, lanes]
            pair = (jnp.where(left2, a, turned(b)), jnp.where(left2, turned(a), b))
            for n in range(2):
                k, c = divmod(2 * p + n, OWN)
                spots = [MSG * k + base + 2 * c]
                if base == 0 and k < NS - 1:
                    spots.append(MSG * (k + 1) + 18 + 2 * c)
                if base == 0 and k > 0:
                    spots.append(MSG * (k - 1) + 24 + 2 * c)
                for spot in spots:
                    msg_out[spot : spot + 2, :] = pair[n]
    for k in range(NS):
        msg_out[MSG * k + 30 : MSG * k + 32, :] = jnp.zeros((2, 128), F32)
    msg_out[18:24, :] = jnp.zeros((6, 128), F32)
    msg_out[MSG * (NS - 1) + 24 : MSG * (NS - 1) + 30, :] = jnp.zeros((6, 128), F32)

    pl.semaphore_wait(barrier, NS + 1)

    def rows_of(ref, k, count):
        return ref.at[pl.ds(pl.multiple_of(count * k, 8), count)]

    def remote(source, target, send, recv, device):
        return pltpu.make_async_remote_copy(source, target, send, recv, device_id=device)

    def small(step, carry):
        k = {"sector": lax.rem(me + step, NS)}
        remote(ids_hbm, ids_all.at[me], ids_sem.at[0], ids_sem.at[1], k).start()
        remote(mist_hbm, mist_all.at[me], mist_sem.at[0], mist_sem.at[1], k).start()
        return carry

    def fields(step, carry):
        k = lax.rem(me + step, NS)
        remote(rows_of(msg_out, k, MSG), rows_of(msg, me, MSG), msg_sem.at[0], msg_sem.at[1], {"sector": k}).start()
        return carry

    lax.fori_loop(1, NS, fields, 0)
    edges = [
        remote(msg_out.at[MSG * (NS - 1) : MSG * (NS - 1) + 8], rows_of(edge, me, 8), edge_send.at[0], edge_recv, {"sector": 0, "dof": dof_up}),
        remote(msg_out.at[0:8], rows_of(edge, me, 8), edge_send.at[1], edge_recv, {"sector": NS - 1, "dof": dof_down}),
    ]
    for copy in edges:
        copy.start()
    lax.fori_loop(1, NS, small, 0)
    msg[pl.ds(pl.multiple_of(MSG * me, 8), MSG), :] = msg_out[pl.ds(pl.multiple_of(MSG * me, 8), MSG), :]

    loads[3].wait()

    def inverse_pair(k, c):
        return jnp.concatenate([inv[0, OWN * k + c], inv[1, OWN * k + c]], axis=1)

    def spread(step, carry):
        k = lax.rem(me + step, NS)
        for c in range(OWN):
            packed[k, c] = inverse_pair(k, c)
        remote(packed.at[k], bulk.at[me], bulk_send, bulk_recv.at[me], {"sector": k}).start()
        return carry

    lax.fori_loop(1, NS, spread, 0)
    for c in range(OWN):
        bulk[me, c] = inverse_pair(me, c)

    loads[4].wait()

    def table(t, carry):
        value = jnp.concatenate([tiles[t], tiles[t]], axis=1)
        high = value.astype(BF16)
        w_table[t, 0:64] = high
        w_table[t, 64:128] = (value - high.astype(F32)).astype(BF16)
        return carry

    lax.fori_loop(0, tiles.shape[0], table, 0, unroll=2)

    loads[5].wait()
    loads[6].wait()
    loads[7].wait()
    nothing = jnp.zeros((64, 64), BF16)
    for c in range(OWN):
        for p in range(4):
            value = stiff[c, p] if p < 3 else coup[c]
            high = value.astype(BF16)
            low = (value - high.astype(F32)).astype(BF16)
            for n, part in enumerate((high, low)):
                lanes = slice(128 * p, 128 * p + 128)
                w_main[c, 128 * n : 128 * n + 64, lanes] = jnp.concatenate([part, nothing], axis=1)
                w_main[c, 128 * n + 64 : 128 * n + 128, lanes] = jnp.concatenate([nothing, part], axis=1)

    def all_rows(ref, sem, count):
        part = ref.at[0 : count * (NS - 1)]
        pltpu.make_async_copy(part, part, sem).wait()

    loads[8].wait()
    all_rows(ids_all, ids_sem.at[1], 1)
    to_ids = pltpu.make_async_copy(ids_all, ids, local_sem.at[10])
    to_ids.start()
    loads[9].wait()
    all_rows(mist_all, mist_sem.at[1], 1)
    to_mist = pltpu.make_async_copy(mist_all, mist, local_sem.at[11])
    to_mist.start()
    to_ids.wait()
    to_mist.wait()

    left128 = iota(128, 1) < 64
    row = iota(8, 0)

    def tile_weights(j, carry):
        factor = jnp.zeros((8, 128), F32)
        for c in range(OWN):
            b = OWN * me + c
            value = jnp.where(left128, w_table[ids[j, 0, b]], w_table[ids[j, 1, b]])
            w_tile[j, :, 128 * c : 128 * c + 128] = value
            for s in range(2):
                factor = jnp.where(row == 2 * c + s, mist[j, s, b], factor)
        scale[pl.ds(pl.multiple_of(8 * j, 8), 8), :] = factor
        return carry

    lax.fori_loop(0, NS, tile_weights, 0)

    all_rows(msg, msg_sem.at[1], MSG)
    for j in range(NS):
        adj[8 * j : 8 * j + 8, :] = msg[MSG * j : MSG * j + 8, :]
        right[8 * j : 8 * j + 8, :] = msg[MSG * j + 6 : MSG * j + 14, :]
        forced[8 * j : 8 * j + 8, :] = msg[MSG * j + 12 : MSG * j + 20, :]
    acc[...] = jnp.zeros(acc.shape, F32)

    def keep(ref, e, value):
        high = value.astype(BF16)
        ref[e, 0:32, :] = high
        ref[e, 32:64, :] = (value - high.astype(F32)).astype(BF16)

    def gathered(ref, r, stride):
        return ref[pl.ds(r, NS, stride=stride), :], ref[pl.ds(r + 1, NS, stride=stride), :]

    def chunk_at(j):
        return pl.ds(pl.multiple_of(8 * j, 8), 8)

    def tile_part(j, carry):
        work[chunk_at(j), :] = right[chunk_at(j), :] - scale[chunk_at(j), :] * own_product(adj[chunk_at(j), :], w_tile[j])
        return carry

    def forced_part(j, carry):
        forced[chunk_at(j), :] = scale[chunk_at(j), :] * own_product(forced[chunk_at(j), :], w_tile[j])
        return carry

    first_block = (dof * NS + me) * OWN - OWN

    def own_blocks(send):
        for c in range(OWN):
            even, odd = gathered(adj, 2 * c, 8)
            own = jnp.concatenate([even, odd], axis=0)
            if send:
                halo_out[32 * c : 32 * c + 32, :] = own
            else:
                keep(wide, OWN + c, own)
                beside = [odd + rolled(odd, 1), even + rolled(even, NS - 1)]
                keep(near, c, jnp.concatenate(beside, axis=0))

    def main_part():
        for c in range(OWN):
            e1 = jnp.maximum(cols[1, OWN * me + c] - first_block, 0)
            e2 = jnp.maximum(cols[2, OWN * me + c] - first_block, 0)
            lhs = jnp.concatenate([wide[OWN + c], wide[e1], wide[e2], near[c]], axis=1)
            out = matmul_t(lhs, w_main[c])
            out = out[0:32] + out[32:64]
            out = out[:, 0:128] + out[:, 128:256]
            acc[pl.ds(2 * c, NS, stride=8), :] = out[0:16]
            acc[pl.ds(2 * c + 1, NS, stride=8), :] = out[16:32]

    def chunks(ref):
        return [ref[8 * j : 8 * j + 8, :] for j in range(NS)]

    def residuals():
        return [w - a for w, a in zip(chunks(work), chunks(acc))]

    def store(ref, values):
        for j in range(NS):
            ref[8 * j : 8 * j + 8, :] = values[j]

    own_blocks(False)
    for c in range(OWN):
        keep(wide, c, jnp.concatenate(gathered(msg, 18 + 2 * c, MSG), axis=0))
        keep(wide, 2 * OWN + c, jnp.concatenate(gathered(msg, 24 + 2 * c, MSG), axis=0))

    @pl.when(me == 0)
    def _():
        pltpu.make_async_copy(edge, edge, edge_recv).wait()
        for c in range(OWN):
            keep(wide, c, jnp.concatenate(gathered(edge, 2 * c, 8), axis=0))

    @pl.when(me == NS - 1)
    def _():
        pltpu.make_async_copy(edge, edge, edge_recv).wait()
        for c in range(OWN):
            keep(wide, 2 * OWN + c, jnp.concatenate(gathered(edge, 2 * c, 8), axis=0))

    lax.fori_loop(0, NS, tile_part, 0, unroll=4)
    main_part()
    store(work, hartley32(residuals()))
    lax.fori_loop(0, NS, forced_part, 0, unroll=4)

    def arrive(step, carry):
        j = lax.rem(me + NS - step, NS)

        @pl.when(step > 0)
        def _():
            pltpu.make_async_copy(bulk.at[j], bulk.at[j], bulk_recv.at[j]).wait()

        for c in range(OWN):
            value = bulk[j, c]
            high = value.astype(BF16)
            lanes = slice(128 * c, 128 * c + 128)
            w_inv[j, 0:64, lanes] = high
            w_inv[j, 64:128, lanes] = (value - high.astype(F32)).astype(BF16)
        acc[chunk_at(j), :] = own_product(work[chunk_at(j), :], w_inv[j])
        return carry

    lax.fori_loop(0, NS, arrive, 0)

    def updated():
        update = hartley32([w * (1.0 / 32.0) for w in chunks(acc)])
        return [a + u for a, u in zip(chunks(adj), update)]

    store(adj, updated())

    own_blocks(True)
    halos = [
        remote(halo_out, halo_low, halo_send.at[0], halo_recv.at[0], up),
        remote(halo_out, halo_high, halo_send.at[1], halo_recv.at[1], down),
    ]
    for copy in halos:
        copy.start()
    own_blocks(False)
    lax.fori_loop(0, NS, tile_part, 0, unroll=4)
    halos[0].wait_recv()
    for c in range(OWN):
        keep(wide, c, halo_low[32 * c : 32 * c + 32, :])
    halos[1].wait_recv()
    for c in range(OWN):
        keep(wide, 2 * OWN + c, halo_high[32 * c : 32 * c + 32, :])
    main_part()
    residual = residuals()
    store(res_out, residual)

    def scatter(source, target, sem):
        def one(step, carry):
            k = lax.rem(me + step, NS)
            remote(rows_of(source, k, 8), rows_of(target, me, 8), sem.at[0], sem.at[1], {"sector": k}).start()
            return carry

        lax.fori_loop(1, NS, one, 0)
        target[chunk_at(me), :] = source[chunk_at(me), :]

    scatter(res_out, res_ref, res_sem)
    store(work, hartley32(residual))

    def solve_part(j, carry):
        acc[chunk_at(j), :] = own_product(work[chunk_at(j), :], w_inv[j])
        return carry

    lax.fori_loop(0, NS, solve_part, 0, unroll=4)
    lane = iota(8, 1)
    for j, value in enumerate(updated()):
        product = value * forced[8 * j : 8 * j + 8, :]
        total = -jnp.sum(product, axis=1, keepdims=True)
        place = jnp.where((lane == OWN * me + row // 2) & (row < 2 * OWN), total, 0.0)
        place = place + rolled(place, 4)
        place = place + rolled(place, 2)
        fin_out[8 * j : 8 * j + 8, :] = jnp.where(row < 2 * OWN, value, place)
    scatter(fin_out, fin_ref, fin_sem)

    for copy in edges + halos:
        copy.wait_send()
    all_rows(ids_all, ids_sem.at[0], 1)
    all_rows(mist_all, mist_sem.at[0], 1)
    all_rows(msg_out, msg_sem.at[0], MSG)
    all_rows(packed, bulk_send, 1)
    all_rows(res_out, res_sem.at[0], 8)
    all_rows(fin_out, fin_sem.at[0], 8)
    all_rows(res_ref, res_sem.at[1], 8)
    all_rows(fin_ref, fin_sem.at[1], 8)


def finish(fin, res, adj_ref, res_ref, sens_ref, other):
    left = iota(2, 1) < 64
    for source, target in ((fin, adj_ref), (res, res_ref)):
        for k in range(NS):
            other[8 * k : 8 * k + 8, :] = turned(source[8 * k : 8 * k + 8, :])
        for p in range(PAIRS):
            spots = [8 * k + 2 * c for k, c in (divmod(2 * p, OWN), divmod(2 * p + 1, OWN))]
            lanes = slice(128 * p, 128 * p + 128)
            for load, (a, b) in enumerate(((source, other), (other, source))):
                target[load, :, lanes] = jnp.where(
                    left, a[spots[0] : spots[0] + 2, :], b[spots[1] : spots[1] + 2, :]
                )
    total = fin[6:8, :]
    for k in range(1, NS):
        total = total + fin[8 * k + 6 : 8 * k + 8, :]
    sens_ref[...] = total[:, : sens_ref.shape[1]]


def body(dof_count, adjoint_start, right_side, response, stiffness, block_cols, coupling, tile_table, tile_ids, mistune, inverses):
    vmem = pl.BlockSpec(memory_space=pltpu.VMEM)
    hbm = pl.BlockSpec(memory_space=pltpu.HBM)
    field = jax.ShapeDtypeStruct(adjoint_start.shape, F32)
    rows = jax.ShapeDtypeStruct((8 * NS, 128), F32)
    chunk_rows = pltpu.VMEM((8 * NS, 128), F32)
    dma = pltpu.SemaphoreType.DMA
    fin, res = pl.pallas_call(
        functools.partial(kernel, dof_count),
        out_shape=(rows, rows),
        in_specs=[hbm] * 10,
        out_specs=(vmem, vmem),
        scratch_shapes=[
            pltpu.VMEM(adjoint_start.shape, F32),
            pltpu.VMEM(adjoint_start.shape, F32),
            pltpu.VMEM(adjoint_start.shape, F32),
            pltpu.SMEM(block_cols.shape[::-1], jnp.int32),
            pltpu.VMEM(tile_table.shape, F32),
            pltpu.VMEM((OWN,) + stiffness.shape[1:], F32),
            pltpu.VMEM((OWN,) + coupling.shape[1:], F32),
            pltpu.VMEM(inverses.shape, F32),
            pltpu.VMEM((NS,) + tile_ids.shape, jnp.int32),
            pltpu.VMEM((NS,) + mistune.shape, F32),
            pltpu.SMEM((NS,) + tile_ids.shape, jnp.int32),
            pltpu.SMEM((NS,) + mistune.shape, F32),
            pltpu.VMEM((MSG * NS, 128), F32),
            pltpu.VMEM((MSG * NS, 128), F32),
            chunk_rows,
            pltpu.VMEM((NS, OWN, 64, 128), F32),
            pltpu.VMEM((NS, OWN, 64, 128), F32),
            pltpu.VMEM((tile_table.shape[0], 128, 128), BF16),
            pltpu.VMEM((NS, 128, OWN * 128), BF16),
            pltpu.VMEM((NS, 128, OWN * 128), BF16),
            pltpu.VMEM((OWN, 256, 512), BF16),
            chunk_rows,
            chunk_rows,
            chunk_rows,
            chunk_rows,
            chunk_rows,
            chunk_rows,
            pltpu.VMEM((3 * OWN, 64, 128), BF16),
            pltpu.VMEM((OWN, 64, 128), BF16),
            pltpu.VMEM((32 * OWN, 128), F32),
            pltpu.VMEM((32 * OWN, 128), F32),
            pltpu.VMEM((32 * OWN, 128), F32),
            chunk_rows,
            chunk_rows,
            dma((12,)),
            dma((2,)),
            dma((2,)),
            dma((2,)),
            dma((2,)),
            dma,
            dma,
            dma((NS,)),
            dma((2,)),
            dma((2,)),
            dma((2,)),
            dma((2,)),
        ],
        compiler_params=pltpu.CompilerParams(collective_id=0, has_side_effects=True, vmem_limit_bytes=60 * 1024 * 1024),
    )(
        adjoint_start, right_side, response, block_cols.T, tile_ids, mistune, stiffness, coupling, tile_table, inverses
    )
    return pl.pallas_call(
        finish,
        out_shape=(field, field, jax.ShapeDtypeStruct(mistune.shape, F32)),
        in_specs=[vmem, vmem],
        out_specs=(vmem, vmem, vmem),
        scratch_shapes=[chunk_rows],
    )(fin, res)


def solution(mesh):
    in_specs = (
        P(None, "sector", "dof"),
        P(None, "sector", "dof"),
        P(None, "sector", "dof"),
        P("dof", None, None, None),
        P("dof", None),
        P("dof", None, None),
        P(),
        P("sector", "dof"),
        P("sector", "dof"),
        P("sector", "dof", None, None),
    )
    out_specs = (P(None, "sector", "dof"), P(None, "sector", "dof"), P("sector", "dof"))
    run = functools.partial(body, mesh.shape["dof"])
    return jax.shard_map(run, mesh=mesh, in_specs=in_specs, out_specs=out_specs, check_vma=False)
```

```python
import functools
import math

import jax
import jax.numpy as jnp
from jax import lax
from jax.experimental import pallas as pl
from jax.experimental.pallas import tpu as pltpu
from jax.sharding import PartitionSpec as P

ITERS = 2
NS = 16
OWN = 3
PAIRS = 24
MSG = 24
F32 = jnp.float32
BF16 = jnp.bfloat16


def iota(rows, axis):
    return lax.broadcasted_iota(jnp.int32, (rows, 128), axis)


def rolled(x, shift):
    return pltpu.roll(x, shift, axis=0)


def turned(x):
    return pltpu.roll(x, 64, axis=1)


def place_of(device):
    x, y = (device // 2) % 2, device // 4
    return 2 * y + device % 2 + x * (14 - 4 * y)


def device_of(place):
    q = place // 2
    h = q // 4
    return 4 * (q + h * (7 - 2 * q)) + 2 * h + place % 2


def hartley16(values):
    count = len(values)
    if count == 1:
        return values
    even, odd = hartley16(values[0::2]), hartley16(values[1::2])
    half = count // 2
    low, high = [], []
    for k in range(half):
        angle = 2.0 * math.pi * k / count
        if k == 0:
            twist = odd[0]
        elif 4 * k == count:
            twist = odd[half - k]
        else:
            twist = math.cos(angle) * odd[k] + math.sin(angle) * odd[half - k]
        low.append(even[k] + twist)
        high.append(even[k] - twist)
    return low + high


def hartley32(values):
    is_even = iota(8, 0) % 2 == 0
    y = hartley16(values)
    twisted = [y[0]]
    for k in range(1, 16):
        angle = 2.0 * math.pi * k / 32
        twisted.append(math.cos(angle) * y[k] + math.sin(angle) * y[16 - k])
    low, high = [], []
    for j in range(8):
        a = jnp.where(is_even, y[2 * j], rolled(y[2 * j + 1], 1))
        b = jnp.where(is_even, rolled(twisted[2 * j], 7), twisted[2 * j + 1])
        low.append(a + b)
        high.append(a - b)
    return low + high


def halves(x):
    high = x.astype(BF16).astype(F32)
    return high, x - high


def matmul_t(a, b):
    return lax.dot_general(a, b, (((1,), (1,)), ((), ())), preferred_element_type=F32)


def spread_rows(x):
    own = (iota(8, 1) // 64) == (iota(8, 0) % 2)
    high0, low0 = halves(jnp.where(own, x, 0.0))
    high1, low1 = halves(jnp.where(own, turned(x), 0.0))
    rows = jnp.concatenate([high0, high1, low0, low1], axis=0)
    block = (iota(32, 0) % 8) // 2
    lhs = [jnp.where(block == c, rows, 0.0).astype(BF16) for c in range(OWN)]
    return jnp.concatenate(lhs, axis=1)


def collected(out):
    own = (iota(8, 1) // 64) == (iota(8, 0) % 2)
    first, second = out[0:8] + out[16:24], out[8:16] + out[24:32]
    return jnp.where(own, first + turned(first), second + turned(second))


def own_product(x, weights):
    return collected(matmul_t(spread_rows(x), weights))


def own_products(x0, x1, weights):
    out = matmul_t(jnp.concatenate([spread_rows(x0), spread_rows(x1)], axis=0), weights)
    return collected(out[0:32, 0:128]), collected(out[32:64, 128:256])


def kernel(
    dof_count,
    v0_hbm, rs_hbm, resp_hbm, cols_hbm, ids_hbm, mist_hbm, stiff_hbm, coup_hbm, tile_hbm, inv_hbm,
    fin_ref,
    v0, rs, resp, cols, tiles, stiff, coup, inv,
    ids_all, mist_all, ids, mist,
    msg_out, msg, edge, packed, bulk,
    w_table, w_tile, w_inv, w_main,
    adj, right, forced, scale, work, acc, wide, near,
    halo_out, halo_low, halo_high, fin_out,
    local_sem, ids_sem, mist_sem, msg_sem, edge_send, edge_recv, bulk_send, bulk_recv,
    halo_send, halo_recv, fin_sem, resp_sem, resp_out,
):
    me = lax.axis_index("sector")
    dof = lax.axis_index("dof")
    place = place_of(me)
    dof_up, dof_down = lax.rem(dof + 1, dof_count), lax.rem(dof + dof_count - 1, dof_count)
    up = {"sector": device_of(lax.rem(place + 1, NS)), "dof": lax.rem(dof + (place + 1) // NS, dof_count)}
    down = {
        "sector": device_of(lax.rem(place + NS - 1, NS)),
        "dof": lax.rem(dof + dof_count - 1 + (place + NS - 1) // NS, dof_count),
    }
    first, last = device_of(0), device_of(NS - 1)

    mine = pl.ds(OWN * place, OWN)
    loads = [
        pltpu.make_async_copy(source, target, local_sem.at[i])
        for i, (source, target) in enumerate(
            (
                (v0_hbm, v0),
                (rs_hbm, rs),
                (resp_hbm, resp),
                (inv_hbm, inv),
                (tile_hbm, tiles),
                (stiff_hbm.at[mine], stiff),
                (coup_hbm.at[mine], coup),
                (cols_hbm, cols),
                (ids_hbm, ids_all.at[me]),
                (mist_hbm, mist_all.at[me]),
            )
        )
    ]

    barrier = pltpu.get_barrier_semaphore()

    def greet(step, carry):
        pl.semaphore_signal(barrier, inc=1, device_id={"sector": lax.rem(me + step, NS)})
        return carry

    for step in (8, 9, 7, 10, 6, 11, 5, 12, 4, 13, 3, 14, 2, 15, 1):
        greet(step, 0)

    def greet_row(row):
        def one(step, carry):
            pl.semaphore_signal(barrier, inc=1, device_id={"sector": step, "dof": row})
            return carry

        lax.fori_loop(0, NS, one, 0)

    @pl.when(place == 0)
    def _():
        greet_row(dof_down)

    @pl.when(place == NS - 1)
    def _():
        greet_row(dof_up)

    for i in (0, 3, 1, 8, 9, 4, 5, 6, 7, 2):
        loads[i].start()

    left2 = iota(2, 1) < 64

    def shape_rows(base, field, target, size):
        for p in range(PAIRS):
            lanes = slice(128 * p, 128 * p + 128)
            a, b = field[0, :, lanes], field[1, :, lanes]
            pair = (jnp.where(left2, a, turned(b)), jnp.where(left2, turned(a), b))
            for n in range(2):
                k, c = divmod(2 * p + n, OWN)
                spots = [size * k + base + 2 * c]
                if field is v0 and k < NS - 1:
                    spots.append(size * (k + 1) + 12 + 2 * c)
                if field is v0 and k > 0:
                    spots.append(size * (k - 1) + 18 + 2 * c)
                for spot in spots:
                    target[spot : spot + 2, :] = pair[n]

    loads[0].wait()
    shape_rows(0, v0, msg_out, MSG)
    loads[1].wait()
    shape_rows(6, rs, msg_out, MSG)
    msg_out[12:18, :] = jnp.zeros((6, 128), F32)
    msg_out[MSG * (NS - 1) + 18 : MSG * (NS - 1) + 24, :] = jnp.zeros((6, 128), F32)

    pl.semaphore_wait(barrier, NS + 1)

    def rows_of(ref, k, count):
        return ref.at[pl.ds(pl.multiple_of(count * k, 8), count)]

    def remote(source, target, send, recv, device):
        return pltpu.make_async_remote_copy(source, target, send, recv, device_id=device)

    def scatter(source, target, sem, count, index=lambda k: k):
        def one(step, carry):
            k = lax.rem(me + step, NS)
            source_rows = rows_of(source, index(k), count)
            remote(source_rows, rows_of(target, me, count), sem.at[0], sem.at[1], {"sector": k}).start()
            return carry

        lax.fori_loop(1, NS, one, 0)
        own_copy = pltpu.make_async_copy(rows_of(source, index(me), count), rows_of(target, me, count), sem.at[2])
        own_copy.start()
        own_copies.append(own_copy)

    own_copies = []

    def small(step, carry):
        k = {"sector": lax.rem(me + step, NS)}
        remote(ids_hbm, ids_all.at[me], ids_sem.at[0], ids_sem.at[1], k).start()
        remote(mist_hbm, mist_all.at[me], mist_sem.at[0], mist_sem.at[1], k).start()
        return carry

    def fields(step, carry):
        k = lax.rem(me + step, NS)
        source = rows_of(msg_out, place_of(k), MSG)
        remote(source, rows_of(msg, me, MSG), msg_sem.at[0], msg_sem.at[1], {"sector": k}).start()
        return carry

    lax.fori_loop(1, NS, fields, 0)
    edges = [
        remote(msg_out.at[MSG * (NS - 1) : MSG * (NS - 1) + 8], rows_of(edge, me, 8), edge_send.at[0], edge_recv, {"sector": first, "dof": dof_up}),
        remote(msg_out.at[0:8], rows_of(edge, me, 8), edge_send.at[1], edge_recv, {"sector": last, "dof": dof_down}),
    ]
    for copy in edges:
        copy.start()
    loads[3].wait()

    def inverse_pair(k, c):
        return jnp.concatenate([inv[0, OWN * place_of(k) + c], inv[1, OWN * place_of(k) + c]], axis=1)

    def spread(step, carry):
        k = lax.rem(me + step, NS)
        for c in range(OWN):
            packed[k, c] = inverse_pair(k, c)
        remote(packed.at[k], bulk.at[me], bulk_send, bulk_recv.at[me], {"sector": k}).start()
        return carry

    lax.fori_loop(1, 4, spread, 0)
    lax.fori_loop(1, NS, small, 0)
    lax.fori_loop(4, NS, spread, 0)
    for c in range(OWN):
        bulk[me, c] = inverse_pair(me, c)
    msg[pl.ds(pl.multiple_of(MSG * me, 8), MSG), :] = msg_out[pl.ds(pl.multiple_of(MSG * place, 8), MSG), :]
    loads[2].wait()
    shape_rows(0, resp, resp_out, 8)
    for k in range(NS):
        resp_out[8 * k + 6 : 8 * k + 8, :] = jnp.zeros((2, 128), F32)
    scatter(resp_out, forced, resp_sem, 8, place_of)

    loads[4].wait()

    def table(t, carry):
        value = jnp.concatenate([tiles[t], tiles[t]], axis=1)
        high = value.astype(BF16)
        w_table[t, 0:64] = high
        w_table[t, 64:128] = (value - high.astype(F32)).astype(BF16)
        return carry

    lax.fori_loop(0, tiles.shape[0], table, 0, unroll=2)

    loads[5].wait()
    loads[6].wait()
    loads[7].wait()
    nothing = jnp.zeros((64, 64), BF16)
    for c in range(OWN):
        for p in range(4):
            value = stiff[c, p] if p < 3 else coup[c]
            high = value.astype(BF16)
            low = (value - high.astype(F32)).astype(BF16)
            for n, part in enumerate((high, low)):
                lanes = slice(128 * p, 128 * p + 128)
                w_main[c, 128 * n : 128 * n + 64, lanes] = jnp.concatenate([part, nothing], axis=1)
                w_main[c, 128 * n + 64 : 128 * n + 128, lanes] = jnp.concatenate([nothing, part], axis=1)

    def all_rows(ref, sem, count):
        part = ref.at[0 : count * (NS - 1)]
        pltpu.make_async_copy(part, part, sem).wait()

    loads[8].wait()
    all_rows(ids_all, ids_sem.at[1], 1)
    to_ids = pltpu.make_async_copy(ids_all, ids, local_sem.at[10])
    to_ids.start()
    loads[9].wait()
    all_rows(mist_all, mist_sem.at[1], 1)
    to_mist = pltpu.make_async_copy(mist_all, mist, local_sem.at[11])
    to_mist.start()
    to_ids.wait()
    to_mist.wait()

    left128 = iota(128, 1) < 64
    row = iota(8, 0)

    def tile_weights(j, carry):
        factor = jnp.zeros((8, 128), F32)
        for c in range(OWN):
            b = OWN * place + c
            value = jnp.where(left128, w_table[ids[j, 0, b]], w_table[ids[j, 1, b]])
            w_tile[j // 2, pl.ds(pl.multiple_of(128 * (j % 2), 128), 128), 128 * c : 128 * c + 128] = value
            for s in range(2):
                factor = jnp.where(row == 2 * c + s, mist[j, s, b], factor)
        scale[pl.ds(pl.multiple_of(8 * j, 8), 8), :] = factor
        return carry

    lax.fori_loop(0, NS, tile_weights, 0)

    all_rows(msg, msg_sem.at[1], MSG)
    for j in range(NS):
        adj[8 * j : 8 * j + 8, :] = msg[MSG * j : MSG * j + 8, :]
        right[8 * j : 8 * j + 8, :] = msg[MSG * j + 6 : MSG * j + 14, :]
    acc[...] = jnp.zeros(acc.shape, F32)

    def keep(ref, e, value):
        high = value.astype(BF16)
        ref[e, 0:32, :] = high
        ref[e, 32:64, :] = (value - high.astype(F32)).astype(BF16)

    def gathered(ref, r, stride):
        return ref[pl.ds(r, NS, stride=stride), :], ref[pl.ds(r + 1, NS, stride=stride), :]

    def chunk_at(j):
        return pl.ds(pl.multiple_of(8 * j, 8), 8)

    def two_chunks(i):
        return chunk_at(2 * i), chunk_at(2 * i + 1)

    def tile_part(i, carry):
        at = two_chunks(i)
        for a, product in zip(at, own_products(adj[at[0], :], adj[at[1], :], w_tile[i])):
            work[a, :] = right[a, :] - scale[a, :] * product
        return carry

    def forced_part(i, carry):
        at = two_chunks(i)
        for a, product in zip(at, own_products(forced[at[0], :], forced[at[1], :], w_tile[i])):
            forced[a, :] = scale[a, :] * product
        return carry

    first_block = (dof * NS + place) * OWN - OWN

    def own_blocks(send):
        for c in range(OWN):
            even, odd = gathered(adj, 2 * c, 8)
            own = jnp.concatenate([even, odd], axis=0)
            if send:
                halo_out[32 * c : 32 * c + 32, :] = own
            else:
                keep(wide, OWN + c, own)
                beside = [odd + rolled(odd, 1), even + rolled(even, NS - 1)]
                keep(near, c, jnp.concatenate(beside, axis=0))

    def main_part():
        for c in range(OWN):
            e1 = jnp.maximum(cols[1, OWN * place + c] - first_block, 0)
            e2 = jnp.maximum(cols[2, OWN * place + c] - first_block, 0)
            lhs = jnp.concatenate([wide[OWN + c], wide[e1], wide[e2], near[c]], axis=1)
            out = matmul_t(lhs, w_main[c])
            out = out[0:32] + out[32:64]
            out = out[:, 0:128] + out[:, 128:256]
            acc[pl.ds(2 * c, NS, stride=8), :] = out[0:16]
            acc[pl.ds(2 * c + 1, NS, stride=8), :] = out[16:32]

    def chunks(ref):
        return [ref[8 * j : 8 * j + 8, :] for j in range(NS)]

    def residuals():
        return [w - a for w, a in zip(chunks(work), chunks(acc))]

    def store(ref, values):
        for j in range(NS):
            ref[8 * j : 8 * j + 8, :] = values[j]

    own_blocks(False)
    for c in range(OWN):
        keep(wide, c, jnp.concatenate(gathered(msg, 12 + 2 * c, MSG), axis=0))
        keep(wide, 2 * OWN + c, jnp.concatenate(gathered(msg, 18 + 2 * c, MSG), axis=0))

    @pl.when(place == 0)
    def _():
        pltpu.make_async_copy(edge, edge, edge_recv).wait()
        for c in range(OWN):
            keep(wide, c, jnp.concatenate(gathered(edge, 2 * c, 8), axis=0))

    @pl.when(place == NS - 1)
    def _():
        pltpu.make_async_copy(edge, edge, edge_recv).wait()
        for c in range(OWN):
            keep(wide, 2 * OWN + c, jnp.concatenate(gathered(edge, 2 * c, 8), axis=0))

    lax.fori_loop(0, NS // 2, tile_part, 0, unroll=4)
    main_part()
    store(work, hartley32(residuals()))

    def arrive(step, carry):
        j = lax.rem(me + NS - step, NS)

        @pl.when(step > 0)
        def _():
            pltpu.make_async_copy(bulk.at[j], bulk.at[j], bulk_recv.at[j]).wait()

        half = pl.multiple_of(128 * (j % 2), 128)
        for c in range(OWN):
            value = bulk[j, c]
            high = value.astype(BF16)
            lanes = slice(128 * c, 128 * c + 128)
            w_inv[j // 2, pl.ds(half, 64), lanes] = high
            w_inv[j // 2, pl.ds(half + 64, 64), lanes] = (value - high.astype(F32)).astype(BF16)
        acc[chunk_at(j), :] = own_product(work[chunk_at(j), :], w_inv[j // 2, pl.ds(half, 128), :])
        return carry

    lax.fori_loop(0, NS, arrive, 0)

    def updated():
        update = hartley32([w * (1.0 / 32.0) for w in chunks(acc)])
        return [a + u for a, u in zip(chunks(adj), update)]

    store(adj, updated())

    own_blocks(True)
    halos = [
        remote(halo_out, halo_low, halo_send.at[0], halo_recv.at[0], up),
        remote(halo_out, halo_high, halo_send.at[1], halo_recv.at[1], down),
    ]
    for copy in halos:
        copy.start()
    own_blocks(False)
    lax.fori_loop(0, NS // 2, tile_part, 0, unroll=4)
    own_copies[0].wait()
    all_rows(forced, resp_sem.at[1], 8)
    lax.fori_loop(0, NS // 2, forced_part, 0, unroll=4)
    halos[0].wait_recv()
    for c in range(OWN):
        keep(wide, c, halo_low[32 * c : 32 * c + 32, :])
    halos[1].wait_recv()
    for c in range(OWN):
        keep(wide, 2 * OWN + c, halo_high[32 * c : 32 * c + 32, :])
    main_part()
    residual = residuals()
    for j in range(NS):
        fin_out[16 * j + 8 : 16 * j + 16, :] = residual[j]

    store(work, hartley32(residual))

    def solve_part(i, carry):
        at = two_chunks(i)
        for a, product in zip(at, own_products(work[at[0], :], work[at[1], :], w_inv[i])):
            acc[a, :] = product
        return carry

    lax.fori_loop(0, NS // 2, solve_part, 0, unroll=8)
    lane = iota(8, 1)
    for j, value in enumerate(updated()):
        product = value * forced[8 * j : 8 * j + 8, :]
        total = -jnp.sum(product, axis=1, keepdims=True)
        spread_out = jnp.where((lane == OWN * place + row // 2) & (row < 2 * OWN), total, 0.0)
        spread_out = spread_out + rolled(spread_out, 4)
        spread_out = spread_out + rolled(spread_out, 2)
        fin_out[16 * j : 16 * j + 8, :] = jnp.where(row < 2 * OWN, value, spread_out)
    scatter(fin_out, fin_ref, fin_sem, 16)

    for copy in edges + halos:
        copy.wait_send()
    for copy in own_copies[1:]:
        copy.wait()
    all_rows(resp_out, resp_sem.at[0], 8)
    all_rows(ids_all, ids_sem.at[0], 1)
    all_rows(mist_all, mist_sem.at[0], 1)
    all_rows(msg_out, msg_sem.at[0], MSG)
    all_rows(packed, bulk_send, 1)
    all_rows(fin_out, fin_sem.at[0], 16)
    all_rows(fin_ref, fin_sem.at[1], 16)


def finish(fin, adj_ref, res_ref, sens_ref, other):
    left = iota(2, 1) < 64
    for k in range(2 * NS):
        other[8 * k : 8 * k + 8, :] = turned(fin[8 * k : 8 * k + 8, :])
    for base, target in ((0, adj_ref), (8, res_ref)):
        for p in range(PAIRS):
            spots = [16 * device_of(k) + base + 2 * c for k, c in (divmod(2 * p, OWN), divmod(2 * p + 1, OWN))]
            lanes = slice(128 * p, 128 * p + 128)
            for load, (a, b) in enumerate(((fin, other), (other, fin))):
                target[load, :, lanes] = jnp.where(
                    left, a[spots[0] : spots[0] + 2, :], b[spots[1] : spots[1] + 2, :]
                )
    total = fin[6:8, :]
    for k in range(1, NS):
        total = total + fin[16 * k + 6 : 16 * k + 8, :]
    sens_ref[...] = total[:, : sens_ref.shape[1]]


def body(dof_count, adjoint_start, right_side, response, stiffness, block_cols, coupling, tile_table, tile_ids, mistune, inverses):
    vmem = pl.BlockSpec(memory_space=pltpu.VMEM)
    hbm = pl.BlockSpec(memory_space=pltpu.HBM)
    field = jax.ShapeDtypeStruct(adjoint_start.shape, F32)
    rows = jax.ShapeDtypeStruct((16 * NS, 128), F32)
    chunk_rows = pltpu.VMEM((8 * NS, 128), F32)
    dma = pltpu.SemaphoreType.DMA
    fin = pl.pallas_call(
        functools.partial(kernel, dof_count),
        out_shape=rows,
        in_specs=[hbm] * 10,
        out_specs=hbm,
        scratch_shapes=[
            pltpu.VMEM(adjoint_start.shape, F32),
            pltpu.VMEM(adjoint_start.shape, F32),
            pltpu.VMEM(adjoint_start.shape, F32),
            pltpu.SMEM(block_cols.shape[::-1], jnp.int32),
            pltpu.VMEM(tile_table.shape, F32),
            pltpu.VMEM((OWN,) + stiffness.shape[1:], F32),
            pltpu.VMEM((OWN,) + coupling.shape[1:], F32),
            pltpu.VMEM(inverses.shape, F32),
            pltpu.VMEM((NS,) + tile_ids.shape, jnp.int32),
            pltpu.VMEM((NS,) + mistune.shape, F32),
            pltpu.SMEM((NS,) + tile_ids.shape, jnp.int32),
            pltpu.SMEM((NS,) + mistune.shape, F32),
            pltpu.VMEM((MSG * NS, 128), F32),
            pltpu.VMEM((MSG * NS, 128), F32),
            chunk_rows,
            pltpu.VMEM((NS, OWN, 64, 128), F32),
            pltpu.VMEM((NS, OWN, 64, 128), F32),
            pltpu.VMEM((tile_table.shape[0], 128, 128), BF16),
            pltpu.VMEM((NS // 2, 256, OWN * 128), BF16),
            pltpu.VMEM((NS // 2, 256, OWN * 128), BF16),
            pltpu.VMEM((OWN, 256, 512), BF16),
            chunk_rows,
            chunk_rows,
            chunk_rows,
            chunk_rows,
            chunk_rows,
            chunk_rows,
            pltpu.VMEM((3 * OWN, 64, 128), BF16),
            pltpu.VMEM((OWN, 64, 128), BF16),
            pltpu.VMEM((32 * OWN, 128), F32),
            pltpu.VMEM((32 * OWN, 128), F32),
            pltpu.VMEM((32 * OWN, 128), F32),
            pltpu.VMEM((16 * NS, 128), F32),
            dma((12,)),
            dma((2,)),
            dma((2,)),
            dma((2,)),
            dma((2,)),
            dma,
            dma,
            dma((NS,)),
            dma((2,)),
            dma((2,)),
            dma((3,)),
            dma((3,)),
            chunk_rows,
        ],
        compiler_params=pltpu.CompilerParams(collective_id=0, has_side_effects=True, vmem_limit_bytes=60 * 1024 * 1024),
    )(
        adjoint_start, right_side, response, block_cols.T, tile_ids, mistune, stiffness, coupling, tile_table, inverses
    )
    return pl.pallas_call(
        finish,
        out_shape=(field, field, jax.ShapeDtypeStruct(mistune.shape, F32)),
        in_specs=[vmem],
        out_specs=(vmem, vmem, vmem),
        scratch_shapes=[pltpu.VMEM((16 * NS, 128), F32)],
    )(fin)


def solution(mesh):
    in_specs = (
        P(None, "sector", "dof"),
        P(None, "sector", "dof"),
        P(None, "sector", "dof"),
        P("dof", None, None, None),
        P("dof", None),
        P("dof", None, None),
        P(),
        P("sector", "dof"),
        P("sector", "dof"),
        P("sector", "dof", None, None),
    )
    out_specs = (P(None, "sector", "dof"), P(None, "sector", "dof"), P("sector", "dof"))
    run = functools.partial(body, mesh.shape["dof"])
    return jax.shard_map(run, mesh=mesh, in_specs=in_specs, out_specs=out_specs, check_vma=False)
```

```python
import functools
import math

import jax
import jax.numpy as jnp
from jax import lax
from jax.experimental import pallas as pl
from jax.experimental.pallas import tpu as pltpu
from jax.sharding import PartitionSpec as P

ITERS = 2
NS = 16
OWN = 3
PAIRS = 24
MSG = 16
F32 = jnp.float32
BF16 = jnp.bfloat16


def iota(rows, axis):
    return lax.broadcasted_iota(jnp.int32, (rows, 128), axis)


def rolled(x, shift):
    return pltpu.roll(x, shift, axis=0)


def turned(x):
    return pltpu.roll(x, 64, axis=1)


def place_of(device):
    x, y = (device // 2) % 2, device // 4
    return 2 * y + device % 2 + x * (14 - 4 * y)


def device_of(place):
    q = place // 2
    h = q // 4
    return 4 * (q + h * (7 - 2 * q)) + 2 * h + place % 2


def hartley16(values):
    count = len(values)
    if count == 1:
        return values
    even, odd = hartley16(values[0::2]), hartley16(values[1::2])
    half = count // 2
    low, high = [], []
    for k in range(half):
        angle = 2.0 * math.pi * k / count
        if k == 0:
            twist = odd[0]
        elif 4 * k == count:
            twist = odd[half - k]
        else:
            twist = math.cos(angle) * odd[k] + math.sin(angle) * odd[half - k]
        low.append(even[k] + twist)
        high.append(even[k] - twist)
    return low + high


def hartley32(values):
    is_even = iota(8, 0) % 2 == 0
    y = hartley16(values)
    twisted = [y[0]]
    for k in range(1, 16):
        angle = 2.0 * math.pi * k / 32
        twisted.append(math.cos(angle) * y[k] + math.sin(angle) * y[16 - k])
    low, high = [], []
    for j in range(8):
        a = jnp.where(is_even, y[2 * j], rolled(y[2 * j + 1], 1))
        b = jnp.where(is_even, rolled(twisted[2 * j], 7), twisted[2 * j + 1])
        low.append(a + b)
        high.append(a - b)
    return low + high


def halves(x):
    high = x.astype(BF16).astype(F32)
    return high, x - high


def matmul_t(a, b):
    return lax.dot_general(a, b, (((1,), (1,)), ((), ())), preferred_element_type=F32)


def own_product(x, weights):
    own = (iota(8, 1) // 64) == (iota(8, 0) % 2)
    high0, low0 = halves(jnp.where(own, x, 0.0))
    high1, low1 = halves(jnp.where(own, turned(x), 0.0))
    rows = jnp.concatenate([high0, high1, low0, low1], axis=0)
    block = (iota(32, 0) % 8) // 2
    lhs = [jnp.where(block == c, rows, 0.0).astype(BF16) for c in range(OWN)]
    out = matmul_t(jnp.concatenate(lhs, axis=1), weights)
    first, second = out[0:8] + out[16:24], out[8:16] + out[24:32]
    return jnp.where(own, first + turned(first), second + turned(second))


def kernel(
    dof_count,
    v0_hbm, rs_hbm, resp_hbm, cols_hbm, ids_hbm, mist_hbm, stiff_hbm, coup_hbm, tile_hbm, inv_hbm,
    fin_ref, forced_ref,
    v0, rs, resp, cols, tiles, stiff, coup, inv,
    ids_all, mist_all, ids, mist,
    msg_out, msg, packed, bulk,
    w_table, w_tile, w_inv, w_main,
    adj, right, forced, scale, work, acc, wide, near,
    halo_out, halo_low, halo_high, fin_out,
    local_sem, ids_sem, mist_sem, msg_sem, bulk_send, bulk_recv,
    halo_send, halo_recv, fin_sem, resp_sem, resp_out,
):
    me = lax.axis_index("sector")
    dof = lax.axis_index("dof")
    place = place_of(me)
    up = {"sector": device_of(lax.rem(place + 1, NS)), "dof": lax.rem(dof + (place + 1) // NS, dof_count)}
    down = {
        "sector": device_of(lax.rem(place + NS - 1, NS)),
        "dof": lax.rem(dof + dof_count - 1 + (place + NS - 1) // NS, dof_count),
    }

    mine = pl.ds(OWN * place, OWN)
    loads = [
        pltpu.make_async_copy(source, target, local_sem.at[i])
        for i, (source, target) in enumerate(
            (
                (v0_hbm, v0),
                (rs_hbm, rs),
                (resp_hbm, resp),
                (inv_hbm, inv),
                (tile_hbm, tiles),
                (stiff_hbm.at[mine], stiff),
                (coup_hbm.at[mine], coup),
                (cols_hbm, cols),
                (ids_hbm, ids_all.at[me]),
                (mist_hbm, mist_all.at[me]),
            )
        )
    ]
    for i in (0, 3, 1, 8, 9, 4, 5, 6, 7, 2):
        loads[i].start()

    barrier = pltpu.get_barrier_semaphore()

    def greet(step, carry):
        pl.semaphore_signal(barrier, inc=1, device_id={"sector": lax.rem(me + step, NS)})
        return carry

    lax.fori_loop(1, NS, greet, 0)
    pl.semaphore_signal(barrier, inc=1, device_id=up)
    pl.semaphore_signal(barrier, inc=1, device_id=down)

    left2 = iota(2, 1) < 64

    def shape_rows(base, field, target, size):
        for p in range(PAIRS):
            lanes = slice(128 * p, 128 * p + 128)
            a, b = field[0, :, lanes], field[1, :, lanes]
            pair = (jnp.where(left2, a, turned(b)), jnp.where(left2, turned(a), b))
            for n in range(2):
                k, c = divmod(2 * p + n, OWN)
                spot = size * k + base + 2 * c
                target[spot : spot + 2, :] = pair[n]

    loads[0].wait()
    shape_rows(0, v0, msg_out, MSG)
    loads[1].wait()
    shape_rows(6, rs, msg_out, MSG)
    for k in range(NS):
        msg_out[MSG * k + 12 : MSG * k + 16, :] = jnp.zeros((4, 128), F32)

    pl.semaphore_wait(barrier, NS + 1)

    def rows_of(ref, k, count):
        return ref.at[pl.ds(pl.multiple_of(count * k, 8), count)]

    def remote(source, target, send, recv, device):
        return pltpu.make_async_remote_copy(source, target, send, recv, device_id=device)

    def scatter(source, target, sem, count, index=lambda k: k):
        def one(step, carry):
            k = lax.rem(me + step, NS)
            source_rows = rows_of(source, index(k), count)
            remote(source_rows, rows_of(target, me, count), sem.at[0], sem.at[1], {"sector": k}).start()
            return carry

        lax.fori_loop(1, NS, one, 0)
        own_copy = pltpu.make_async_copy(rows_of(source, index(me), count), rows_of(target, me, count), sem.at[2])
        own_copy.start()
        own_copies.append(own_copy)

    own_copies = []

    def all_rows(ref, sem, count):
        part = ref.at[0 : count * (NS - 1)]
        pltpu.make_async_copy(part, part, sem).wait()

    def gathered(ref, r):
        return ref[pl.ds(r, NS, stride=8), :], ref[pl.ds(r + 1, NS, stride=8), :]

    def start_halo(it):
        for c in range(OWN):
            halo_out[it, 32 * c : 32 * c + 32, :] = jnp.concatenate(gathered(adj, 2 * c), axis=0)
        copies = [
            remote(halo_out.at[it], halo_low.at[it], halo_send.at[it, 0], halo_recv.at[it, 0], up),
            remote(halo_out.at[it], halo_high.at[it], halo_send.at[it, 1], halo_recv.at[it, 1], down),
        ]
        for copy in copies:
            copy.start()
        return copies

    def small(step, carry):
        k = {"sector": lax.rem(me + step, NS)}
        remote(ids_hbm, ids_all.at[me], ids_sem.at[0], ids_sem.at[1], k).start()
        remote(mist_hbm, mist_all.at[me], mist_sem.at[0], mist_sem.at[1], k).start()
        return carry

    def fields(step, carry):
        k = lax.rem(me + step, NS)
        source = rows_of(msg_out, place_of(k), MSG)
        remote(source, rows_of(msg, me, MSG), msg_sem.at[0], msg_sem.at[1], {"sector": k}).start()
        return carry

    lax.fori_loop(1, NS, fields, 0)
    lax.fori_loop(1, NS, small, 0)
    loads[3].wait()

    def inverse_pair(k, c):
        return jnp.concatenate([inv[0, OWN * place_of(k) + c], inv[1, OWN * place_of(k) + c]], axis=1)

    def spread(step, carry):
        k = lax.rem(me + step, NS)
        for c in range(OWN):
            packed[k, c] = inverse_pair(k, c)
        remote(packed.at[k], bulk.at[me], bulk_send, bulk_recv.at[me], {"sector": k}).start()
        return carry

    lax.fori_loop(1, 4, spread, 0)
    lax.fori_loop(4, 15, spread, 0)
    msg[pl.ds(pl.multiple_of(MSG * me, 8), MSG), :] = msg_out[pl.ds(pl.multiple_of(MSG * place, 8), MSG), :]
    all_rows(msg, msg_sem.at[1], MSG)
    for j in range(NS):
        adj[8 * j : 8 * j + 8, :] = msg[MSG * j : MSG * j + 8, :]
    halos = start_halo(0)
    lax.fori_loop(15, NS, spread, 0)
    for c in range(OWN):
        bulk[me, c] = inverse_pair(me, c)
    for j in range(NS):
        right[8 * j : 8 * j + 8, :] = msg[MSG * j + 6 : MSG * j + 14, :]
    acc[...] = jnp.zeros(acc.shape, F32)

    loads[4].wait()

    def table(t, carry):
        value = jnp.concatenate([tiles[t], tiles[t]], axis=1)
        high = value.astype(BF16)
        w_table[t, 0:64] = high
        w_table[t, 64:128] = (value - high.astype(F32)).astype(BF16)
        return carry

    lax.fori_loop(0, tiles.shape[0], table, 0, unroll=2)

    loads[5].wait()
    loads[6].wait()
    loads[7].wait()
    nothing = jnp.zeros((64, 64), BF16)
    for c in range(OWN):
        for p in range(4):
            value = stiff[c, p] if p < 3 else coup[c]
            high = value.astype(BF16)
            low = (value - high.astype(F32)).astype(BF16)
            for n, part in enumerate((high, low)):
                lanes = slice(128 * p, 128 * p + 128)
                w_main[c, 128 * n : 128 * n + 64, lanes] = jnp.concatenate([part, nothing], axis=1)
                w_main[c, 128 * n + 64 : 128 * n + 128, lanes] = jnp.concatenate([nothing, part], axis=1)

    loads[8].wait()
    all_rows(ids_all, ids_sem.at[1], 1)
    to_ids = pltpu.make_async_copy(ids_all, ids, local_sem.at[10])
    to_ids.start()
    loads[9].wait()
    all_rows(mist_all, mist_sem.at[1], 1)
    to_mist = pltpu.make_async_copy(mist_all, mist, local_sem.at[11])
    to_mist.start()
    to_ids.wait()
    to_mist.wait()

    left128 = iota(128, 1) < 64
    row = iota(8, 0)

    def tile_weights(j, carry):
        factor = jnp.zeros((8, 128), F32)
        for c in range(OWN):
            b = OWN * place + c
            value = jnp.where(left128, w_table[ids[j, 0, b]], w_table[ids[j, 1, b]])
            w_tile[j, :, 128 * c : 128 * c + 128] = value
            for s in range(2):
                factor = jnp.where(row == 2 * c + s, mist[j, s, b], factor)
        scale[pl.ds(pl.multiple_of(8 * j, 8), 8), :] = factor
        return carry

    lax.fori_loop(0, NS, tile_weights, 0)

    def keep(ref, e, value):
        high = value.astype(BF16)
        ref[e, 0:32, :] = high
        ref[e, 32:64, :] = (value - high.astype(F32)).astype(BF16)

    def chunk_at(j):
        return pl.ds(pl.multiple_of(8 * j, 8), 8)

    def tile_part(j, carry):
        work[chunk_at(j), :] = right[chunk_at(j), :] - scale[chunk_at(j), :] * own_product(adj[chunk_at(j), :], w_tile[j])
        return carry

    def forced_part(p, carry):
        factor = jnp.zeros((8, 128), F32)
        weights = []
        for c in range(OWN):
            b = OWN * p + c
            weights.append(jnp.where(left128, w_table[ids[me, 0, b]], w_table[ids[me, 1, b]]))
            for s in range(2):
                factor = jnp.where(row == 2 * c + s, mist[me, s, b], factor)
        product = own_product(resp_out[chunk_at(p), :], jnp.concatenate(weights, axis=1))
        forced[chunk_at(p), :] = factor * product
        return carry

    first_block = (dof * NS + place) * OWN - OWN

    def own_blocks():
        for c in range(OWN):
            even, odd = gathered(adj, 2 * c)
            keep(wide, OWN + c, jnp.concatenate([even, odd], axis=0))
            beside = [odd + rolled(odd, 1), even + rolled(even, NS - 1)]
            keep(near, c, jnp.concatenate(beside, axis=0))

    def finish_halo(it, copies):
        for copy, target, e in ((copies[0], halo_low, 0), (copies[1], halo_high, 2 * OWN)):
            copy.wait_recv()
            for c in range(OWN):
                keep(wide, e + c, target[it, 32 * c : 32 * c + 32, :])

    def main_part():
        for c in range(OWN):
            e1 = jnp.maximum(cols[1, OWN * place + c] - first_block, 0)
            e2 = jnp.maximum(cols[2, OWN * place + c] - first_block, 0)
            lhs = jnp.concatenate([wide[OWN + c], wide[e1], wide[e2], near[c]], axis=1)
            out = matmul_t(lhs, w_main[c])
            out = out[0:32] + out[32:64]
            out = out[:, 0:128] + out[:, 128:256]
            acc[pl.ds(2 * c, NS, stride=8), :] = out[0:16]
            acc[pl.ds(2 * c + 1, NS, stride=8), :] = out[16:32]

    def chunks(ref):
        return [ref[8 * j : 8 * j + 8, :] for j in range(NS)]

    def residuals():
        return [w - a for w, a in zip(chunks(work), chunks(acc))]

    def store(ref, values):
        for j in range(NS):
            ref[8 * j : 8 * j + 8, :] = values[j]

    def split_inverses(j):
        for c in range(OWN):
            value = bulk[j, c]
            high = value.astype(BF16)
            lanes = slice(128 * c, 128 * c + 128)
            w_inv[j, 0:64, lanes] = high
            w_inv[j, 64:128, lanes] = (value - high.astype(F32)).astype(BF16)

    def accept(step, carry):
        j = lax.rem(me + NS - step, NS)
        pltpu.make_async_copy(bulk.at[j], bulk.at[j], bulk_recv.at[j]).wait()
        split_inverses(j)
        return carry

    def solve_part(j, carry):
        acc[chunk_at(j), :] = own_product(work[chunk_at(j), :], w_inv[j])
        return carry

    def solve_early(step, carry):
        return solve_part(lax.rem(me + NS - step, NS), carry)

    def arrive(step, carry):
        accept(step, carry)
        return solve_early(step, carry)

    own_blocks()
    lax.fori_loop(0, NS, tile_part, 0, unroll=8)
    loads[2].wait()
    shape_rows(0, resp, resp_out, 8)
    for k in range(NS):
        resp_out[8 * k + 6 : 8 * k + 8, :] = jnp.zeros((2, 128), F32)
    lax.fori_loop(0, NS, forced_part, 0, unroll=4)
    own_copies.append(pltpu.make_async_copy(forced, forced_ref, resp_sem))
    own_copies[0].start()
    split_inverses(me)
    lax.fori_loop(1, 10, accept, 0)
    finish_halo(0, halos)
    main_part()
    store(work, hartley32(residuals()))
    lax.fori_loop(0, 10, solve_early, 0, unroll=10 // 2)
    lax.fori_loop(10, NS, arrive, 0)

    def updated():
        update = hartley32([w * (1.0 / 32.0) for w in chunks(acc)])
        return [a + u for a, u in zip(chunks(adj), update)]

    store(adj, updated())

    halos += start_halo(1)
    own_blocks()
    lax.fori_loop(0, NS, tile_part, 0, unroll=8)
    finish_halo(1, halos[2:])
    main_part()
    residual = residuals()
    for j in range(NS):
        fin_out[16 * j + 8 : 16 * j + 16, :] = residual[j]

    store(work, hartley32(residual))

    lax.fori_loop(0, NS, solve_part, 0, unroll=16)
    for j, value in enumerate(updated()):
        fin_out[16 * j : 16 * j + 8, :] = value
    scatter(fin_out, fin_ref, fin_sem, 16)

    for copy in halos:
        copy.wait_send()
    for copy in own_copies:
        copy.wait()
    all_rows(ids_all, ids_sem.at[0], 1)
    all_rows(mist_all, mist_sem.at[0], 1)
    all_rows(msg_out, msg_sem.at[0], MSG)
    all_rows(packed, bulk_send, 1)
    all_rows(fin_out, fin_sem.at[0], 16)
    all_rows(fin_ref, fin_sem.at[1], 16)


def finish(fin, forced, adj_ref, res_ref, sens_ref, other):
    left = iota(2, 1) < 64
    for k in range(2 * NS):
        other[8 * k : 8 * k + 8, :] = turned(fin[8 * k : 8 * k + 8, :])
    for base, target in ((0, adj_ref), (8, res_ref)):
        for p in range(PAIRS):
            spots = [16 * device_of(k) + base + 2 * c for k, c in (divmod(2 * p, OWN), divmod(2 * p + 1, OWN))]
            lanes = slice(128 * p, 128 * p + 128)
            for load, (a, b) in enumerate(((fin, other), (other, fin))):
                target[load, :, lanes] = jnp.where(
                    left, a[spots[0] : spots[0] + 2, :], b[spots[1] : spots[1] + 2, :]
                )
    lane, row = iota(8, 1), iota(8, 0)
    sens = jnp.zeros((8, 128), F32)
    for k in range(NS):
        p = place_of(k)
        product = fin[16 * k : 16 * k + 8, :] * forced[8 * p : 8 * p + 8, :]
        total = -jnp.sum(product, axis=1, keepdims=True)
        sens = jnp.where((lane == OWN * p + row // 2) & (row < 2 * OWN), total, sens)
    sens = sens + rolled(sens, 4)
    sens = sens + rolled(sens, 2)
    sens_ref[...] = sens[6:8, : sens_ref.shape[1]]


def body(dof_count, adjoint_start, right_side, response, stiffness, block_cols, coupling, tile_table, tile_ids, mistune, inverses):
    vmem = pl.BlockSpec(memory_space=pltpu.VMEM)
    hbm = pl.BlockSpec(memory_space=pltpu.HBM)
    field = jax.ShapeDtypeStruct(adjoint_start.shape, F32)
    rows = jax.ShapeDtypeStruct((16 * NS, 128), F32)
    chunk_rows = pltpu.VMEM((8 * NS, 128), F32)
    dma = pltpu.SemaphoreType.DMA
    fin, forced = pl.pallas_call(
        functools.partial(kernel, dof_count),
        out_shape=(rows, jax.ShapeDtypeStruct((8 * NS, 128), F32)),
        in_specs=[hbm] * 10,
        out_specs=(hbm, hbm),
        scratch_shapes=[
            pltpu.VMEM(adjoint_start.shape, F32),
            pltpu.VMEM(adjoint_start.shape, F32),
            pltpu.VMEM(adjoint_start.shape, F32),
            pltpu.SMEM(block_cols.shape[::-1], jnp.int32),
            pltpu.VMEM(tile_table.shape, F32),
            pltpu.VMEM((OWN,) + stiffness.shape[1:], F32),
            pltpu.VMEM((OWN,) + coupling.shape[1:], F32),
            pltpu.VMEM(inverses.shape, F32),
            pltpu.VMEM((NS,) + tile_ids.shape, jnp.int32),
            pltpu.VMEM((NS,) + mistune.shape, F32),
            pltpu.SMEM((NS,) + tile_ids.shape, jnp.int32),
            pltpu.SMEM((NS,) + mistune.shape, F32),
            pltpu.VMEM((MSG * NS, 128), F32),
            pltpu.VMEM((MSG * NS, 128), F32),
            pltpu.VMEM((NS, OWN, 64, 128), F32),
            pltpu.VMEM((NS, OWN, 64, 128), F32),
            pltpu.VMEM((tile_table.shape[0], 128, 128), BF16),
            pltpu.VMEM((NS, 128, OWN * 128), BF16),
            pltpu.VMEM((NS, 128, OWN * 128), BF16),
            pltpu.VMEM((OWN, 256, 512), BF16),
            chunk_rows,
            chunk_rows,
            chunk_rows,
            chunk_rows,
            chunk_rows,
            chunk_rows,
            pltpu.VMEM((3 * OWN, 64, 128), BF16),
            pltpu.VMEM((OWN, 64, 128), BF16),
            pltpu.VMEM((ITERS, 32 * OWN, 128), F32),
            pltpu.VMEM((ITERS, 32 * OWN, 128), F32),
            pltpu.VMEM((ITERS, 32 * OWN, 128), F32),
            pltpu.VMEM((16 * NS, 128), F32),
            dma((12,)),
            dma((2,)),
            dma((2,)),
            dma((2,)),
            dma,
            dma((NS,)),
            dma((ITERS, 2)),
            dma((ITERS, 2)),
            dma((3,)),
            dma,
            chunk_rows,
        ],
        compiler_params=pltpu.CompilerParams(collective_id=0, has_side_effects=True, vmem_limit_bytes=60 * 1024 * 1024),
    )(
        adjoint_start, right_side, response, block_cols.T, tile_ids, mistune, stiffness, coupling, tile_table, inverses
    )
    return pl.pallas_call(
        finish,
        out_shape=(field, field, jax.ShapeDtypeStruct(mistune.shape, F32)),
        in_specs=[vmem, vmem],
        out_specs=(vmem, vmem, vmem),
        scratch_shapes=[pltpu.VMEM((16 * NS, 128), F32)],
    )(fin, forced)


def solution(mesh):
    in_specs = (
        P(None, "sector", "dof"),
        P(None, "sector", "dof"),
        P(None, "sector", "dof"),
        P("dof", None, None, None),
        P("dof", None),
        P("dof", None, None),
        P(),
        P("sector", "dof"),
        P("sector", "dof"),
        P("sector", "dof", None, None),
    )
    out_specs = (P(None, "sector", "dof"), P(None, "sector", "dof"), P("sector", "dof"))
    run = functools.partial(body, mesh.shape["dof"])
    return jax.shard_map(run, mesh=mesh, in_specs=in_specs, out_specs=out_specs, check_vma=False)
```

```python
import functools
import math

import jax
import jax.numpy as jnp
from jax import lax
from jax.experimental import pallas as pl
from jax.experimental.pallas import tpu as pltpu
from jax.sharding import PartitionSpec as P

ITERS = 2
NS = 16
OWN = 3
PAIRS = 24
MSG = 24
ORDER = (1, 4, 12, 5, 13, 2, 8, 3, 9, 6, 14, 7, 15, 10, 11)
F32 = jnp.float32
BF16 = jnp.bfloat16


def iota(rows, axis):
    return lax.broadcasted_iota(jnp.int32, (rows, 128), axis)


def rolled(x, shift):
    return pltpu.roll(x, shift, axis=0)


def turned(x):
    return pltpu.roll(x, 64, axis=1)


def place_of(device):
    x, y = (device // 2) % 2, device // 4
    return 2 * y + device % 2 + x * (14 - 4 * y)


def device_of(place):
    q = place // 2
    h = q // 4
    return 4 * (q + h * (7 - 2 * q)) + 2 * h + place % 2


def hartley16(values):
    count = len(values)
    if count == 1:
        return values
    even, odd = hartley16(values[0::2]), hartley16(values[1::2])
    half = count // 2
    low, high = [], []
    for k in range(half):
        angle = 2.0 * math.pi * k / count
        if k == 0:
            twist = odd[0]
        elif 4 * k == count:
            twist = odd[half - k]
        else:
            twist = math.cos(angle) * odd[k] + math.sin(angle) * odd[half - k]
        low.append(even[k] + twist)
        high.append(even[k] - twist)
    return low + high


def hartley32(values):
    is_even = iota(8, 0) % 2 == 0
    y = hartley16(values)
    twisted = [y[0]]
    for k in range(1, 16):
        angle = 2.0 * math.pi * k / 32
        twisted.append(math.cos(angle) * y[k] + math.sin(angle) * y[16 - k])
    low, high = [], []
    for j in range(8):
        a = jnp.where(is_even, y[2 * j], rolled(y[2 * j + 1], 1))
        b = jnp.where(is_even, rolled(twisted[2 * j], 7), twisted[2 * j + 1])
        low.append(a + b)
        high.append(a - b)
    return low + high


def halves(x):
    high = x.astype(BF16).astype(F32)
    return high, x - high


def matmul_t(a, b):
    return lax.dot_general(a, b, (((1,), (1,)), ((), ())), preferred_element_type=F32)


def spread_rows(x):
    own = (iota(8, 1) // 64) == (iota(8, 0) % 2)
    high0, low0 = halves(jnp.where(own, x, 0.0))
    high1, low1 = halves(jnp.where(own, turned(x), 0.0))
    rows = jnp.concatenate([high0, high1, low0, low1], axis=0)
    block = (iota(32, 0) % 8) // 2
    lhs = [jnp.where(block == c, rows, 0.0).astype(BF16) for c in range(OWN)]
    return jnp.concatenate(lhs, axis=1)


def collected(out):
    own = (iota(8, 1) // 64) == (iota(8, 0) % 2)
    first, second = out[0:8] + out[16:24], out[8:16] + out[24:32]
    return jnp.where(own, first + turned(first), second + turned(second))


def own_product(x, weights):
    return collected(matmul_t(spread_rows(x), weights))


def own_products(x0, x1, weights):
    out = matmul_t(jnp.concatenate([spread_rows(x0), spread_rows(x1)], axis=0), weights)
    return collected(out[0:32, 0:128]), collected(out[32:64, 128:256])


def kernel(
    dof_count,
    v0_hbm, rs_hbm, resp_hbm, cols_hbm, ids_hbm, mist_hbm, stiff_hbm, coup_hbm, tile_hbm, inv_hbm,
    fin_ref, forced_ref,
    v0, rs, resp, cols, tiles, stiff, coup, inv,
    ids_all, mist_all, ids, mist,
    msg_out, msg, edge, packed, bulk,
    w_table, w_tile, w_inv, w_main,
    adj, right, forced, scale, work, acc, wide, near,
    halo_out, halo_low, halo_high, fin_out,
    local_sem, ids_sem, mist_sem, msg_sem, edge_send, edge_recv, bulk_send, bulk_recv,
    halo_send, halo_recv, fin_sem, resp_sem, resp_out,
):
    me = lax.axis_index("sector")
    dof = lax.axis_index("dof")
    place = place_of(me)
    y, x, core = me // 4, lax.rem(me // 2, 2), lax.rem(me, 2)

    def peer(t, way):
        far = lax.rem(y + (t // 4 if way > 0 else 4 - t // 4), 4)
        return 4 * far + 2 * lax.rem(x + (t // 2) % 2, 2) + lax.rem(core + t % 2, 2)

    dof_up, dof_down = lax.rem(dof + 1, dof_count), lax.rem(dof + dof_count - 1, dof_count)
    up = {"sector": device_of(lax.rem(place + 1, NS)), "dof": lax.rem(dof + (place + 1) // NS, dof_count)}
    down = {
        "sector": device_of(lax.rem(place + NS - 1, NS)),
        "dof": lax.rem(dof + dof_count - 1 + (place + NS - 1) // NS, dof_count),
    }
    first, last = device_of(0), device_of(NS - 1)

    mine = pl.ds(OWN * place, OWN)
    loads = [
        pltpu.make_async_copy(source, target, local_sem.at[i])
        for i, (source, target) in enumerate(
            (
                (v0_hbm, v0),
                (rs_hbm, rs),
                (resp_hbm, resp),
                (inv_hbm, inv),
                (tile_hbm, tiles),
                (stiff_hbm.at[mine], stiff),
                (coup_hbm.at[mine], coup),
                (cols_hbm, cols),
                (ids_hbm, ids_all.at[me]),
                (mist_hbm, mist_all.at[me]),
            )
        )
    ]

    barrier = pltpu.get_barrier_semaphore()

    def greet(step, carry):
        pl.semaphore_signal(barrier, inc=1, device_id={"sector": lax.rem(me + step, NS)})
        return carry

    for step in (8, 9, 7, 10, 6, 11, 5, 12, 4, 13, 3, 14, 2, 15, 1):
        greet(step, 0)

    def greet_row(row):
        def one(step, carry):
            pl.semaphore_signal(barrier, inc=1, device_id={"sector": step, "dof": row})
            return carry

        lax.fori_loop(0, NS, one, 0)

    @pl.when(place == 0)
    def _():
        greet_row(dof_down)

    @pl.when(place == NS - 1)
    def _():
        greet_row(dof_up)

    for i in (0, 3, 1, 8, 9, 4, 5, 6, 7, 2):
        loads[i].start()

    left2 = iota(2, 1) < 64

    def shape_rows(base, field, target, size):
        for p in range(PAIRS):
            lanes = slice(128 * p, 128 * p + 128)
            a, b = field[0, :, lanes], field[1, :, lanes]
            pair = (jnp.where(left2, a, turned(b)), jnp.where(left2, turned(a), b))
            for n in range(2):
                k, c = divmod(2 * p + n, OWN)
                spots = [size * k + base + 2 * c]
                if field is v0 and k < NS - 1:
                    spots.append(size * (k + 1) + 12 + 2 * c)
                if field is v0 and k > 0:
                    spots.append(size * (k - 1) + 18 + 2 * c)
                for spot in spots:
                    target[spot : spot + 2, :] = pair[n]

    loads[0].wait()
    shape_rows(0, v0, msg_out, MSG)
    loads[1].wait()
    shape_rows(6, rs, msg_out, MSG)
    msg_out[12:18, :] = jnp.zeros((6, 128), F32)
    msg_out[MSG * (NS - 1) + 18 : MSG * (NS - 1) + 24, :] = jnp.zeros((6, 128), F32)

    pl.semaphore_wait(barrier, NS + 1)

    def rows_of(ref, k, count):
        return ref.at[pl.ds(pl.multiple_of(count * k, 8), count)]

    def remote(source, target, send, recv, device):
        return pltpu.make_async_remote_copy(source, target, send, recv, device_id=device)

    def scatter(source, target, sem, count, index=lambda k: k):
        def one(step, carry):
            k = lax.rem(me + step, NS)
            source_rows = rows_of(source, index(k), count)
            remote(source_rows, rows_of(target, me, count), sem.at[0], sem.at[1], {"sector": k}).start()
            return carry

        lax.fori_loop(1, NS, one, 0)
        own_copy = pltpu.make_async_copy(rows_of(source, index(me), count), rows_of(target, me, count), sem.at[2])
        own_copy.start()
        own_copies.append(own_copy)

    own_copies = []

    def small(step, carry):
        k = {"sector": lax.rem(me + step, NS)}
        remote(ids_hbm, ids_all.at[me], ids_sem.at[0], ids_sem.at[1], k).start()
        remote(mist_hbm, mist_all.at[me], mist_sem.at[0], mist_sem.at[1], k).start()
        return carry

    def fields(step, carry):
        k = lax.rem(me + step, NS)
        source = rows_of(msg_out, place_of(k), MSG)
        remote(source, rows_of(msg, me, MSG), msg_sem.at[0], msg_sem.at[1], {"sector": k}).start()
        return carry

    lax.fori_loop(1, NS, fields, 0)
    edges = [
        remote(msg_out.at[MSG * (NS - 1) : MSG * (NS - 1) + 8], rows_of(edge, me, 8), edge_send.at[0], edge_recv, {"sector": first, "dof": dof_up}),
        remote(msg_out.at[0:8], rows_of(edge, me, 8), edge_send.at[1], edge_recv, {"sector": last, "dof": dof_down}),
    ]
    for copy in edges:
        copy.start()
    loads[3].wait()

    def inverse_pair(k, c):
        return jnp.concatenate([inv[0, OWN * place_of(k) + c], inv[1, OWN * place_of(k) + c]], axis=1)

    def spread(step, carry):
        k = peer(step, 1)
        for c in range(OWN):
            packed[k, c] = inverse_pair(k, c)
        remote(packed.at[k], bulk.at[me], bulk_send, bulk_recv.at[me], {"sector": k}).start()
        return carry

    for t in ORDER[:3]:
        spread(t, 0)
    lax.fori_loop(1, NS, small, 0)
    for t in ORDER[3:]:
        spread(t, 0)
    for c in range(OWN):
        bulk[me, c] = inverse_pair(me, c)
    msg[pl.ds(pl.multiple_of(MSG * me, 8), MSG), :] = msg_out[pl.ds(pl.multiple_of(MSG * place, 8), MSG), :]

    loads[4].wait()

    def table(t, carry):
        value = jnp.concatenate([tiles[t], tiles[t]], axis=1)
        high = value.astype(BF16)
        w_table[t, 0:64] = high
        w_table[t, 64:128] = (value - high.astype(F32)).astype(BF16)
        return carry

    lax.fori_loop(0, tiles.shape[0], table, 0, unroll=2)

    loads[5].wait()
    loads[6].wait()
    loads[7].wait()
    nothing = jnp.zeros((64, 64), BF16)
    for c in range(OWN):
        for p in range(4):
            value = stiff[c, p] if p < 3 else coup[c]
            high = value.astype(BF16)
            low = (value - high.astype(F32)).astype(BF16)
            for n, part in enumerate((high, low)):
                lanes = slice(128 * p, 128 * p + 128)
                w_main[c, 128 * n : 128 * n + 64, lanes] = jnp.concatenate([part, nothing], axis=1)
                w_main[c, 128 * n + 64 : 128 * n + 128, lanes] = jnp.concatenate([nothing, part], axis=1)

    def all_rows(ref, sem, count):
        part = ref.at[0 : count * (NS - 1)]
        pltpu.make_async_copy(part, part, sem).wait()

    loads[8].wait()
    all_rows(ids_all, ids_sem.at[1], 1)
    to_ids = pltpu.make_async_copy(ids_all, ids, local_sem.at[10])
    to_ids.start()
    loads[9].wait()
    all_rows(mist_all, mist_sem.at[1], 1)
    to_mist = pltpu.make_async_copy(mist_all, mist, local_sem.at[11])
    to_mist.start()
    to_ids.wait()
    to_mist.wait()

    left128 = iota(128, 1) < 64
    row = iota(8, 0)

    def tile_weights(j, carry):
        factor = jnp.zeros((8, 128), F32)
        for c in range(OWN):
            b = OWN * place + c
            value = jnp.where(left128, w_table[ids[j, 0, b]], w_table[ids[j, 1, b]])
            w_tile[j // 2, pl.ds(pl.multiple_of(128 * (j % 2), 128), 128), 128 * c : 128 * c + 128] = value
            for s in range(2):
                factor = jnp.where(row == 2 * c + s, mist[j, s, b], factor)
        scale[pl.ds(pl.multiple_of(8 * j, 8), 8), :] = factor
        return carry

    lax.fori_loop(0, NS, tile_weights, 0)

    all_rows(msg, msg_sem.at[1], MSG)
    for j in range(NS):
        adj[8 * j : 8 * j + 8, :] = msg[MSG * j : MSG * j + 8, :]
        right[8 * j : 8 * j + 8, :] = msg[MSG * j + 6 : MSG * j + 14, :]
    acc[...] = jnp.zeros(acc.shape, F32)

    def keep(ref, e, value):
        high = value.astype(BF16)
        ref[e, 0:32, :] = high
        ref[e, 32:64, :] = (value - high.astype(F32)).astype(BF16)

    def gathered(ref, r, stride):
        return ref[pl.ds(r, NS, stride=stride), :], ref[pl.ds(r + 1, NS, stride=stride), :]

    def chunk_at(j):
        return pl.ds(pl.multiple_of(8 * j, 8), 8)

    def two_chunks(i):
        return chunk_at(2 * i), chunk_at(2 * i + 1)

    def tile_part(i, carry):
        at = two_chunks(i)
        for a, product in zip(at, own_products(adj[at[0], :], adj[at[1], :], w_tile[i])):
            work[a, :] = right[a, :] - scale[a, :] * product
        return carry

    def forced_part(p, carry):
        factor = jnp.zeros((8, 128), F32)
        weights = []
        for c in range(OWN):
            b = OWN * p + c
            weights.append(jnp.where(left128, w_table[ids[me, 0, b]], w_table[ids[me, 1, b]]))
            for s in range(2):
                factor = jnp.where(row == 2 * c + s, mist[me, s, b], factor)
        product = own_product(resp_out[chunk_at(p), :], jnp.concatenate(weights, axis=1))
        forced[chunk_at(p), :] = factor * product
        return carry

    first_block = (dof * NS + place) * OWN - OWN

    def own_blocks(send):
        for c in range(OWN):
            even, odd = gathered(adj, 2 * c, 8)
            own = jnp.concatenate([even, odd], axis=0)
            if send:
                halo_out[32 * c : 32 * c + 32, :] = own
            else:
                keep(wide, OWN + c, own)
                beside = [odd + rolled(odd, 1), even + rolled(even, NS - 1)]
                keep(near, c, jnp.concatenate(beside, axis=0))

    def main_part():
        for c in range(OWN):
            e1 = jnp.maximum(cols[1, OWN * place + c] - first_block, 0)
            e2 = jnp.maximum(cols[2, OWN * place + c] - first_block, 0)
            lhs = jnp.concatenate([wide[OWN + c], wide[e1], wide[e2], near[c]], axis=1)
            out = matmul_t(lhs, w_main[c])
            out = out[0:32] + out[32:64]
            out = out[:, 0:128] + out[:, 128:256]
            acc[pl.ds(2 * c, NS, stride=8), :] = out[0:16]
            acc[pl.ds(2 * c + 1, NS, stride=8), :] = out[16:32]

    def chunks(ref):
        return [ref[8 * j : 8 * j + 8, :] for j in range(NS)]

    def residuals():
        return [w - a for w, a in zip(chunks(work), chunks(acc))]

    def store(ref, values):
        for j in range(NS):
            ref[8 * j : 8 * j + 8, :] = values[j]

    own_blocks(False)
    for c in range(OWN):
        keep(wide, c, jnp.concatenate(gathered(msg, 12 + 2 * c, MSG), axis=0))
        keep(wide, 2 * OWN + c, jnp.concatenate(gathered(msg, 18 + 2 * c, MSG), axis=0))

    @pl.when(place == 0)
    def _():
        pltpu.make_async_copy(edge, edge, edge_recv).wait()
        for c in range(OWN):
            keep(wide, c, jnp.concatenate(gathered(edge, 2 * c, 8), axis=0))

    @pl.when(place == NS - 1)
    def _():
        pltpu.make_async_copy(edge, edge, edge_recv).wait()
        for c in range(OWN):
            keep(wide, 2 * OWN + c, jnp.concatenate(gathered(edge, 2 * c, 8), axis=0))

    lax.fori_loop(0, NS // 2, tile_part, 0, unroll=4)
    main_part()
    store(work, hartley32(residuals()))

    def arrive(step, carry):
        j = peer(step, -1) if step else me
        if step:
            pltpu.make_async_copy(bulk.at[j], bulk.at[j], bulk_recv.at[j]).wait()

        half = pl.multiple_of(128 * (j % 2), 128)
        for c in range(OWN):
            value = bulk[j, c]
            high = value.astype(BF16)
            lanes = slice(128 * c, 128 * c + 128)
            w_inv[j // 2, pl.ds(half, 64), lanes] = high
            w_inv[j // 2, pl.ds(half + 64, 64), lanes] = (value - high.astype(F32)).astype(BF16)
        acc[chunk_at(j), :] = own_product(work[chunk_at(j), :], w_inv[j // 2, pl.ds(half, 128), :])
        return carry

    loads[2].wait()
    shape_rows(0, resp, resp_out, 8)
    for k in range(NS):
        resp_out[8 * k + 6 : 8 * k + 8, :] = jnp.zeros((2, 128), F32)
    lax.fori_loop(0, NS, forced_part, 0, unroll=4)
    own_copies.append(pltpu.make_async_copy(forced, forced_ref, resp_sem))
    own_copies[0].start()
    for t in (0,) + ORDER:
        arrive(t, 0)

    def updated():
        update = hartley32([w * (1.0 / 32.0) for w in chunks(acc)])
        return [a + u for a, u in zip(chunks(adj), update)]

    store(adj, updated())

    own_blocks(True)
    halos = [
        remote(halo_out, halo_low, halo_send.at[0], halo_recv.at[0], up),
        remote(halo_out, halo_high, halo_send.at[1], halo_recv.at[1], down),
    ]
    for copy in halos:
        copy.start()
    own_blocks(False)
    lax.fori_loop(0, NS // 2, tile_part, 0, unroll=4)
    halos[0].wait_recv()
    for c in range(OWN):
        keep(wide, c, halo_low[32 * c : 32 * c + 32, :])
    halos[1].wait_recv()
    for c in range(OWN):
        keep(wide, 2 * OWN + c, halo_high[32 * c : 32 * c + 32, :])
    main_part()
    residual = residuals()
    for j in range(NS):
        fin_out[16 * j + 8 : 16 * j + 16, :] = residual[j]

    store(work, hartley32(residual))

    def solve_part(i, carry):
        at = two_chunks(i)
        for a, product in zip(at, own_products(work[at[0], :], work[at[1], :], w_inv[i])):
            acc[a, :] = product
        return carry

    lax.fori_loop(0, NS // 2, solve_part, 0, unroll=8)
    for j, value in enumerate(updated()):
        fin_out[16 * j : 16 * j + 8, :] = value
    scatter(fin_out, fin_ref, fin_sem, 16)

    for copy in edges + halos:
        copy.wait_send()
    for copy in own_copies:
        copy.wait()
    all_rows(ids_all, ids_sem.at[0], 1)
    all_rows(mist_all, mist_sem.at[0], 1)
    all_rows(msg_out, msg_sem.at[0], MSG)
    all_rows(packed, bulk_send, 1)
    all_rows(fin_out, fin_sem.at[0], 16)
    all_rows(fin_ref, fin_sem.at[1], 16)


def finish(fin, forced, adj_ref, res_ref, sens_ref, other):
    left = iota(2, 1) < 64
    for k in range(2 * NS):
        other[8 * k : 8 * k + 8, :] = turned(fin[8 * k : 8 * k + 8, :])
    for base, target in ((0, adj_ref), (8, res_ref)):
        for p in range(PAIRS):
            spots = [16 * device_of(k) + base + 2 * c for k, c in (divmod(2 * p, OWN), divmod(2 * p + 1, OWN))]
            lanes = slice(128 * p, 128 * p + 128)
            for load, (a, b) in enumerate(((fin, other), (other, fin))):
                target[load, :, lanes] = jnp.where(
                    left, a[spots[0] : spots[0] + 2, :], b[spots[1] : spots[1] + 2, :]
                )
    lane, row = iota(8, 1), iota(8, 0)
    sens = jnp.zeros((8, 128), F32)
    for k in range(NS):
        p = place_of(k)
        product = fin[16 * k : 16 * k + 8, :] * forced[8 * p : 8 * p + 8, :]
        total = -jnp.sum(product, axis=1, keepdims=True)
        sens = jnp.where((lane == OWN * p + row // 2) & (row < 2 * OWN), total, sens)
    sens = sens + rolled(sens, 4)
    sens = sens + rolled(sens, 2)
    sens_ref[...] = sens[6:8, : sens_ref.shape[1]]


def body(dof_count, adjoint_start, right_side, response, stiffness, block_cols, coupling, tile_table, tile_ids, mistune, inverses):
    vmem = pl.BlockSpec(memory_space=pltpu.VMEM)
    hbm = pl.BlockSpec(memory_space=pltpu.HBM)
    field = jax.ShapeDtypeStruct(adjoint_start.shape, F32)
    rows = jax.ShapeDtypeStruct((16 * NS, 128), F32)
    chunk_rows = pltpu.VMEM((8 * NS, 128), F32)
    dma = pltpu.SemaphoreType.DMA
    fin, forced = pl.pallas_call(
        functools.partial(kernel, dof_count),
        out_shape=(rows, jax.ShapeDtypeStruct((8 * NS, 128), F32)),
        in_specs=[hbm] * 10,
        out_specs=(hbm, hbm),
        scratch_shapes=[
            pltpu.VMEM(adjoint_start.shape, F32),
            pltpu.VMEM(adjoint_start.shape, F32),
            pltpu.VMEM(adjoint_start.shape, F32),
            pltpu.SMEM(block_cols.shape[::-1], jnp.int32),
            pltpu.VMEM(tile_table.shape, F32),
            pltpu.VMEM((OWN,) + stiffness.shape[1:], F32),
            pltpu.VMEM((OWN,) + coupling.shape[1:], F32),
            pltpu.VMEM(inverses.shape, F32),
            pltpu.VMEM((NS,) + tile_ids.shape, jnp.int32),
            pltpu.VMEM((NS,) + mistune.shape, F32),
            pltpu.SMEM((NS,) + tile_ids.shape, jnp.int32),
            pltpu.SMEM((NS,) + mistune.shape, F32),
            pltpu.VMEM((MSG * NS, 128), F32),
            pltpu.VMEM((MSG * NS, 128), F32),
            chunk_rows,
            pltpu.VMEM((NS, OWN, 64, 128), F32),
            pltpu.VMEM((NS, OWN, 64, 128), F32),
            pltpu.VMEM((tile_table.shape[0], 128, 128), BF16),
            pltpu.VMEM((NS // 2, 256, OWN * 128), BF16),
            pltpu.VMEM((NS // 2, 256, OWN * 128), BF16),
            pltpu.VMEM((OWN, 256, 512), BF16),
            chunk_rows,
            chunk_rows,
            chunk_rows,
            chunk_rows,
            chunk_rows,
            chunk_rows,
            pltpu.VMEM((3 * OWN, 64, 128), BF16),
            pltpu.VMEM((OWN, 64, 128), BF16),
            pltpu.VMEM((32 * OWN, 128), F32),
            pltpu.VMEM((32 * OWN, 128), F32),
            pltpu.VMEM((32 * OWN, 128), F32),
            pltpu.VMEM((16 * NS, 128), F32),
            dma((12,)),
            dma((2,)),
            dma((2,)),
            dma((2,)),
            dma((2,)),
            dma,
            dma,
            dma((NS,)),
            dma((2,)),
            dma((2,)),
            dma((3,)),
            dma,
            chunk_rows,
        ],
        compiler_params=pltpu.CompilerParams(collective_id=0, has_side_effects=True, vmem_limit_bytes=60 * 1024 * 1024),
    )(
        adjoint_start, right_side, response, block_cols.T, tile_ids, mistune, stiffness, coupling, tile_table, inverses
    )
    return pl.pallas_call(
        finish,
        out_shape=(field, field, jax.ShapeDtypeStruct(mistune.shape, F32)),
        in_specs=[vmem, vmem],
        out_specs=(vmem, vmem, vmem),
        scratch_shapes=[pltpu.VMEM((16 * NS, 128), F32)],
    )(fin, forced)


def solution(mesh):
    in_specs = (
        P(None, "sector", "dof"),
        P(None, "sector", "dof"),
        P(None, "sector", "dof"),
        P("dof", None, None, None),
        P("dof", None),
        P("dof", None, None),
        P(),
        P("sector", "dof"),
        P("sector", "dof"),
        P("sector", "dof", None, None),
    )
    out_specs = (P(None, "sector", "dof"), P(None, "sector", "dof"), P("sector", "dof"))
    run = functools.partial(body, mesh.shape["dof"])
    return jax.shard_map(run, mesh=mesh, in_specs=in_specs, out_specs=out_specs, check_vma=False)
```
